32 devices in a mesh: energy: 8 (over z, y), slab: 4 (over x, core).
Axes of the slice: x: 2, y: 2, z: 4, core: 2. Of those that a mesh axis runs over, the one named last changes fastest.
Arguments:
- green_prev: bfloat16 [8, 4, 2, 512, 512], P('energy', 'slab'), may hold values from -6 to 6
- slab_inverse: bfloat16 [4, 2, 512, 512], P('slab')
- coupling_block: bfloat16 [512, 512], replicated
- phonon_coupling: bfloat16 [4, 512, 512], P(None, 'energy'), may hold values from -0.1796875 to 0.1796875
- offset: float32 [8], P('energy'), may hold values from -0.5 to 0.5
- occupation: float32 [8], P('energy'), may hold values from 0.05 to 1
- pair_source: int32 [8, 6], replicated, may hold values from 0 to 7
- pair_mode: int32 [8, 6], replicated, may hold values from 0 to 3
- active_slabs: int32 [8], P('energy'), may hold values from 1 to 4, as said below
Outputs:
- green_new: bfloat16 [8, 4, 2, 512, 512], P('energy', 'slab')
- density: float32 [4, 512], P('slab')
The draws below stay inside these ranges and needn't reach their ends.
Inputs may be any that keep to these rules, and one draw needn't show every extreme that they name: `active_slabs`: some energy scatters in all 4 slabs.
All inputs are finite; a program needn't handle non-finite values.
Results may differ from the reference program's by a relative error of at most 0.012.
Values may be sent and summed in bfloat16 or wider, within the bound.
No kernel may reach another device: no remote copies, remote signals or barrier semaphores. Data moves between devices by JAX's collectives and lax.ppermute only.
A program may use at most 128 MiB of HBM per device.

```python
import math
import jax
import jax.numpy as jnp
import numpy as np
from jax import lax

ORBITALS = 512
MODES = 4
PAIRS = 6
ENERGIES = 8
SLABS = 4


def draw_slab_inverse(key, part):
    key_list = jax.random.split(key, 3)
    shape_full = (SLABS, ORBITALS, ORBITALS)
    noise_real = jax.random.normal(key_list[0], shape_full, jnp.float32)
    noise_imag = jax.random.normal(key_list[1], shape_full, jnp.float32)
    spread = 0.3 / math.sqrt(ORBITALS)
    diagonal_gain = jax.random.uniform(key_list[2], (SLABS, ORBITALS), jnp.float32, 0.7, 1.3)
    identity_matrix = jnp.eye(ORBITALS, dtype=jnp.float32)
    real_block = noise_real * spread + diagonal_gain[:, :, None] * identity_matrix[None]
    imag_block = noise_imag * spread
    return jnp.stack((real_block, imag_block), axis=1).astype(jnp.bfloat16)


def draw_coupling_block(key, part):
    key_list = jax.random.split(key, 2)
    noise_block = jax.random.normal(key_list[0], (ORBITALS, ORBITALS), jnp.float32)
    diagonal_gain = jax.random.uniform(key_list[1], (ORBITALS,), jnp.float32, 0.8, 1.2)
    identity_matrix = jnp.eye(ORBITALS, dtype=jnp.float32)
    block_value = 0.55 * diagonal_gain[:, None] * identity_matrix + noise_block * (0.2 / math.sqrt(ORBITALS))
    return block_value.astype(jnp.bfloat16)


def draw_active_slabs(key, part):
    key_list = jax.random.split(key, 2)
    values_drawn = jax.random.randint(key_list[0], (ENERGIES,), 1, SLABS + 1, dtype=jnp.int32)
    chosen = jax.random.randint(key_list[1], (), 0, ENERGIES, dtype=jnp.int32)
    positions = jnp.arange(ENERGIES, dtype=jnp.int32)
    return jnp.where(positions == chosen, jnp.int32(SLABS), values_drawn).astype(jnp.int32)


def touch_ends(entries, key, least, largest):
    spot = [jax.random.randint(jax.random.fold_in(key, axis), (), 0, length) for axis, length in enumerate(entries.shape)]
    widest = entries.shape.index(max(entries.shape))
    next_to = spot[:widest] + [(spot[widest] + 1) % entries.shape[widest]] + spot[widest + 1:]
    return entries.at[tuple(spot)].set(least).at[tuple(next_to)].set(largest)


def block_scale(own_key, extent, cuts, least, high):
    gain = 1.0
    for axis_at, parts in cuts:
        draws = jax.random.uniform(jax.random.fold_in(jax.random.fold_in(own_key, 6), axis_at), (parts,), jnp.float32, least / len(cuts), high / len(cuts))
        gain = gain * jnp.repeat(jnp.exp(draws), extent[axis_at] // parts).reshape((-1,) + (1,) * (len(extent) - 1 - axis_at))
    return gain


def cumulative_ranks(number_of, lean):
    weights = [(1 << 20) // math.isqrt(rank ** lean) + 1 for rank in range(1, number_of + 1)]
    scale = 1 + sum(weights) // (1 << 30)
    return np.cumsum(np.array([max(1, weight // scale) for weight in weights]))


def ranked(key, shape, amount, lean):
    listing = cumulative_ranks(amount, lean)
    lot = jax.random.randint(jax.random.fold_in(key, 1), shape, 0, int(listing[amount - 1]))
    standing = jnp.searchsorted(jnp.asarray(listing, jnp.int32), lot, side="right")
    return jax.random.permutation(jax.random.fold_in(key, 2), amount)[standing].astype(jnp.int32)


def scatter_about(key, shape, width, bound, pieces=(), kind=jnp.bfloat16):
    entries = jax.random.normal(key, shape, jnp.float32) * width
    if len(pieces) > 0:
        entries = block_scale(key, shape, pieces, -0.22, 0.18) * entries
    return jnp.clip(entries, min=-bound, max=bound).astype(kind)


def setup_inputs(seed: int = 0) -> dict:
    key_of = jax.random.split(jax.random.key(seed), 10)
    return {
        "green_prev": scatter_about(key_of[0], (ENERGIES, SLABS, 2, ORBITALS, ORBITALS), 1.0, 6.0, ((0, 8), (1, 4))),
        "slab_inverse": draw_slab_inverse(jax.random.fold_in(key_of[9], 71), 0),
        "coupling_block": draw_coupling_block(jax.random.fold_in(key_of[9], 71), 0),
        "phonon_coupling": scatter_about(key_of[3], (MODES, ORBITALS, ORBITALS), 0.03, 0.1796875, ((1, 8),)),
        "offset": jnp.clip(jax.random.uniform(key_of[4], (ENERGIES,), jnp.float32, -0.5, 0.5) * block_scale(key_of[4], (ENERGIES,), ((0, 8),), -0.4, 0.0), -0.5, 0.5),
        "occupation": jnp.clip(jnp.exp(math.log(1.0) - 2.9957323 * jax.random.uniform(key_of[5], (ENERGIES,), jnp.float32) ** block_scale(key_of[5], (ENERGIES,), ((0, 8),), -0.2, 0.2)), 0.05, 1.0),
        "pair_source": touch_ends(ranked(key_of[6], (ENERGIES, PAIRS), ENERGIES, 1), jax.random.fold_in(key_of[6], 3), 0, ENERGIES - 1).astype(jnp.int32),
        "pair_mode": touch_ends(jax.random.randint(key_of[7], (ENERGIES, PAIRS), 0, MODES), jax.random.fold_in(key_of[7], 1), 0, MODES - 1).astype(jnp.int32),
        "active_slabs": draw_active_slabs(jax.random.fold_in(key_of[9], 71), 0),
    }


def complex_dot(first_real, first_imag, second_real, second_imag):
    real_part = jnp.dot(first_real, second_real, preferred_element_type=jnp.float32) - jnp.dot(first_imag, second_imag, preferred_element_type=jnp.float32)
    imag_part = jnp.dot(first_real, second_imag, preferred_element_type=jnp.float32) + jnp.dot(first_imag, second_real, preferred_element_type=jnp.float32)
    return jnp.stack((real_part, imag_part))


def reference(green_prev, slab_inverse, coupling_block, phonon_coupling, offset, occupation, pair_source, pair_mode, active_slabs):
    energy_iota = jnp.arange(ENERGIES, dtype=jnp.int32)
    mode_iota = jnp.arange(MODES, dtype=jnp.int32)
    source_hot = (pair_source[:, :, None] == energy_iota[None, None, :]).astype(jnp.float32)
    mode_hot = (pair_mode[:, :, None] == mode_iota[None, None, :]).astype(jnp.float32)
    weights = jnp.einsum('epf,epm->mef', source_hot, mode_hot).astype(jnp.bfloat16)

    def mix_slab(green_slab):
        flat_rows = green_slab.reshape(ENERGIES, -1)
        summed = jnp.zeros(green_slab.shape, jnp.float32)
        for mode_index in range(MODES):
            combined = jnp.dot(weights[mode_index], flat_rows, preferred_element_type=jnp.float32).reshape(green_slab.shape)
            summed = summed + phonon_coupling[mode_index].astype(jnp.float32)[None, None] * combined
        return summed.astype(jnp.bfloat16)

    self_energy = jnp.moveaxis(lax.map(mix_slab, jnp.moveaxis(green_prev, 1, 0)), 0, 1)

    def couple_slab(block):
        return jnp.stack((jnp.dot(block[0], coupling_block, preferred_element_type=jnp.float32), jnp.dot(block[1], coupling_block, preferred_element_type=jnp.float32))).astype(jnp.bfloat16)

    couple = lax.map(couple_slab, slab_inverse)
    identity_matrix = jnp.eye(ORBITALS, dtype=jnp.float32)
    slab_iota = jnp.arange(SLABS, dtype=jnp.int32)

    def per_energy(items):
        energy_sigma, energy_offset, energy_active = items

        def advance(carry, slab_items):
            inverse, factor, sigma_block, position = slab_items
            active_mask = (position < energy_active).astype(jnp.float32)
            total_real = active_mask * sigma_block[0].astype(jnp.float32) + energy_offset * identity_matrix
            total_imag = active_mask * sigma_block[1].astype(jnp.float32)
            sig_total = jnp.stack((total_real, total_imag)).astype(jnp.bfloat16)
            half_product = complex_dot(inverse[0], inverse[1], sig_total[0], sig_total[1]).astype(jnp.bfloat16)
            base_block = inverse.astype(jnp.float32) + complex_dot(half_product[0], half_product[1], inverse[0], inverse[1])
            left_block = complex_dot(factor[0], factor[1], carry[0], carry[1]).astype(jnp.bfloat16)
            right_block = complex_dot(left_block[0], left_block[1], factor[0].T, factor[1].T)
            fresh = (right_block + base_block).astype(jnp.bfloat16)
            return fresh, fresh

        start = jnp.zeros((2, ORBITALS, ORBITALS), jnp.bfloat16)
        final_block, blocks = lax.scan(advance, start, (slab_inverse, couple, energy_sigma, slab_iota))
        return blocks

    green_new = lax.map(per_energy, (self_energy, offset, active_slabs))
    diagonal_imag = jnp.diagonal(green_new[:, :, 1].astype(jnp.float32), axis1=-2, axis2=-1)
    density = -jnp.einsum('e,esn->sn', occupation.astype(jnp.float32), diagonal_imag)
    return green_new, density
```

```python
import functools

import jax
import jax.numpy as jnp
from jax import lax
from jax.experimental import pallas as pl
from jax.experimental.pallas import tpu as pltpu
from jax.sharding import PartitionSpec as P

BF16 = jnp.bfloat16
F32 = jnp.float32
VMEM = pl.BlockSpec(memory_space=pltpu.VMEM)
SMEM = pl.BlockSpec(memory_space=pltpu.SMEM)
VMEM_LIMIT = 48 * 2**20


def mxu(first, second):
    return jnp.dot(first, second, preferred_element_type=F32)


def mxu_nt(first, second):
    return lax.dot_general(first, second, (((1,), (1,)), ((), ())), preferred_element_type=F32)


def call(kernel, out_shape, in_specs, scratch=(), flops=0, bytes_accessed=0):
    return pl.pallas_call(
        kernel,
        out_shape=out_shape,
        in_specs=in_specs,
        out_specs=jax.tree.map(lambda _: VMEM, out_shape),
        scratch_shapes=list(scratch),
        compiler_params=pltpu.CompilerParams(vmem_limit_bytes=VMEM_LIMIT),
        cost_estimate=pl.CostEstimate(flops=flops, bytes_accessed=bytes_accessed, transcendentals=0),
    )


def embed_store(ref, column):
    n = column.shape[1]
    real, imag = column[:n], column[n:]
    ref[:n, :n] = real
    ref[n:, n:] = real
    ref[n:, :n] = imag
    ref[:n, n:] = -imag


def mix_kernel(place_ref, source_ref, mode_ref, phonon_ref, *refs):
    energies = (len(refs) - 2) // 2
    pieces, outs = refs[:energies], refs[energies : 2 * energies]
    green, phonon = refs[2 * energies :]
    place = place_ref[0]
    pairs = source_ref.shape[1]
    rows, n = phonon_ref.shape[1:]
    phonon[...] = phonon_ref[...].astype(F32)
    for distance in range(energies):
        green[distance] = pieces[distance][...].astype(F32)
    step = 16

    @pl.loop(0, rows // step)
    def _(block):
        at = pl.ds(pl.multiple_of(block * step, step), step)
        for distance in range(energies):
            energy = place ^ distance
            real = jnp.zeros((step, n), F32)
            imag = jnp.zeros((step, n), F32)
            for pair in range(pairs):
                origin = source_ref[energy, pair] ^ place
                factor = phonon[mode_ref[energy, pair], at, :]
                real = real + factor * green[origin, 0, at, :]
                imag = imag + factor * green[origin, 1, at, :]
            outs[distance][at, :n] = real.astype(BF16)
            outs[distance][at, n:] = imag.astype(BF16)


def mix(place, source, mode, phonon, pieces):
    energies = len(pieces)
    _, rows, n = pieces[0].shape
    return call(
        mix_kernel,
        [jax.ShapeDtypeStruct((rows, 2 * n), BF16)] * energies,
        [SMEM] * 3 + [VMEM] * (energies + 1),
        [pltpu.VMEM((energies, 2, rows, n), F32), pltpu.VMEM(phonon.shape, F32)],
        flops=energies * 24 * rows * n * 16,
        bytes_accessed=energies * rows * n * 8,
    )(place, source, mode, phonon, *pieces)


def right_kernel(place_ref, scalar_ref, right_ref, inverse_ref, *refs):
    pieces, out_ref, rows_ref = refs[:-2], refs[-2], refs[-1]
    count = len(pieces)
    rows = pieces[0].shape[0]
    n = inverse_ref.shape[1]
    base = place_ref[0]
    for index, piece in enumerate(pieces):
        at = (place_ref[1] ^ index) & (count - 1)
        rows_ref[pl.ds(pl.multiple_of(at * rows, rows), rows), :] = piece[...]
    mask, offset = scalar_ref[0], scalar_ref[1]
    start = pl.multiple_of(base * (rows * count), rows * count)
    total = count * rows
    eye = (
        lax.broadcasted_iota(jnp.int32, (total, n), 0) + start
        == lax.broadcasted_iota(jnp.int32, (total, n), 1)
    ).astype(F32)
    for part in range(2):
        product = mxu(rows_ref[...], right_ref[:, part * n : (part + 1) * n])
        own = inverse_ref[part, pl.ds(start, total), :].astype(F32)
        value = mask * product + offset * own
        if part == 0:
            value = value + eye
        out_ref[:, part * n : (part + 1) * n] = value.astype(BF16)


def right_rows(place, scalars, right, inverse, pieces):
    rows = pieces[0].shape[0]
    total = rows * len(pieces)
    n = inverse.shape[1]
    return call(
        right_kernel,
        jax.ShapeDtypeStruct((total, 2 * n), BF16),
        [SMEM, SMEM] + [VMEM] * (2 + len(pieces)),
        [pltpu.VMEM((total, 2 * n), BF16)],
        flops=8 * total * n * n,
        bytes_accessed=8 * n * n,
    )(place, scalars, right, inverse, *pieces)


def own_matrices_kernel(core_ref, low_ref, high_ref, self_ref, coupling_ref, low_col, high_embed, factor_embed):
    n = coupling_ref.shape[0]
    coupling = coupling_ref[...]
    low_col[...] = mxu(low_ref[...], coupling).astype(BF16)
    embed_store(high_embed, mxu(high_ref[...], coupling).astype(BF16))

    @pl.when(core_ref[0] == 0)
    def _():
        embed_store(factor_embed, mxu(high_embed[...], self_ref[...]).astype(BF16))

    @pl.when(core_ref[0] != 0)
    def _():
        factor_embed[...] = jnp.zeros_like(factor_embed)


def own_matrices(core, low, high, own, coupling):
    n = coupling.shape[0]
    square = jax.ShapeDtypeStruct((2 * n, 2 * n), BF16)
    return call(
        own_matrices_kernel,
        [jax.ShapeDtypeStruct((2 * n, n), BF16), square, square],
        [SMEM] + [VMEM] * 4,
        flops=16 * n**3,
        bytes_accessed=28 * n * n,
    )(core, low, high, own, coupling)


def far_matrices_kernel(core_ref, chain_ref, far_high_ref, far_self_ref, coupling_ref, high_embed, moves, factors, embed, column):
    n = coupling_ref.shape[0]
    core = core_ref[0]
    embed_store(embed, chain_ref[...])

    @pl.when(core == 0)
    def _():
        far_high = mxu(far_high_ref[...], coupling_ref[...]).astype(BF16)
        column[...] = mxu(embed[...], far_high).astype(BF16)
        embed_store(embed, column[...])

    @pl.when(core != 0)
    def _():
        column[...] = chain_ref[...]

    low, high = core, 1 - core
    moves[low] = embed[...]
    column[...] = mxu(high_embed[...], column[...]).astype(BF16)
    embed_store(moves.at[high], column[...])
    for place in range(2):
        embed_store(factors.at[place], mxu(moves[place], far_self_ref[...]).astype(BF16))


def far_matrices(core, chain, far_high, far_self, coupling, high_embed):
    n = coupling.shape[0]
    pair = jax.ShapeDtypeStruct((2, 2 * n, 2 * n), BF16)
    return call(
        far_matrices_kernel,
        [pair, pair],
        [SMEM] + [VMEM] * 5,
        [pltpu.VMEM((2 * n, 2 * n), BF16), pltpu.VMEM((2 * n, n), BF16)],
        flops=36 * n**3,
        bytes_accessed=28 * n * n,
    )(core, chain, far_high, far_self, coupling, high_embed)


def left_kernel(bases_ref, *refs, plan, out_index):
    refs = list(refs)
    out_ref, rows_ref, column_ref = refs[-3:]
    n = out_ref.shape[1]
    total = None
    cursor = 0
    for has_move, chunks, index in plan:
        for chunk in range(chunks):
            block = refs[cursor]
            cursor += 1
            size = block.shape[0]
            start = pl.multiple_of(bases_ref[chunk] * size, size)
            rows_ref[pl.ds(start, size), :] = block[...]
        if has_move:
            move = refs[cursor]
            cursor += 1
            move = move if index is None else move.at[index]
            for part in range(2):
                column_ref[part * n : (part + 1) * n, :] = mxu_nt(
                    rows_ref[...], move[part * n : (part + 1) * n, :]
                ).astype(BF16)
        else:
            column_ref[:n, :] = rows_ref[:, :n]
            column_ref[n:, :] = rows_ref[:, n:]
        factor = refs[cursor]
        cursor += 1
        factor = factor if index is None else factor.at[index]
        product = mxu(factor[...], column_ref[...])
        total = product if total is None else total + product
    out_ref[...] = total.astype(out_ref.dtype)


def left_sum(bases, terms, dtype, n):
    plan, arrays = [], []
    for chunks, move, factor, index in terms:
        plan.append((move is not None, len(chunks), index))
        arrays += list(chunks)
        if move is not None:
            arrays.append(move)
        arrays.append(factor)
    return call(
        functools.partial(left_kernel, plan=tuple(plan), out_index=None),
        jax.ShapeDtypeStruct((2 * n, n), dtype),
        [SMEM] + [VMEM] * len(arrays),
        [pltpu.VMEM((n, 2 * n), BF16), pltpu.VMEM((2 * n, n), BF16)],
        flops=16 * n**3 * len(terms),
        bytes_accessed=16 * n * n * len(terms),
    )(bases, *arrays)


def finish_kernel(scalar_ref, own_ref, partner_ref, green_ref, density_ref):
    n = own_ref.shape[1]
    green = (own_ref[...] + partner_ref[...].astype(F32)).astype(BF16)
    green_ref[...] = green
    eye = lax.broadcasted_iota(jnp.int32, (n, n), 0) == lax.broadcasted_iota(jnp.int32, (n, n), 1)
    diagonal = jnp.sum(jnp.where(eye, green[n:].astype(F32), 0.0), axis=0, keepdims=True)
    density_ref[...] = -scalar_ref[0] * diagonal


def finish(scalars, own, partner):
    n = own.shape[1]
    return call(
        finish_kernel,
        [jax.ShapeDtypeStruct((2 * n, n), BF16), jax.ShapeDtypeStruct((1, n), F32)],
        [SMEM, VMEM, VMEM],
        flops=8 * n * n,
        bytes_accessed=16 * n * n,
    )(scalars, own, partner)


def exchange(x, axis, distance):
    size = lax.axis_size(axis)
    return lax.ppermute(x, axis, [(i, i ^ distance) for i in range(size)])


def shift(x, axis, by):
    size = lax.axis_size(axis)
    return lax.ppermute(x, axis, [(i, i + by) for i in range(size - by)])


def local(
    green_prev,
    slab_inverse,
    coupling_block,
    phonon_coupling,
    offset,
    occupation,
    pair_source,
    pair_mode,
    active_slabs,
):
    energies = pair_source.shape[0]
    n = coupling_block.shape[0]
    rows = n // energies
    slabs = lax.axis_size("slab")
    place = lax.axis_index("energy").astype(jnp.int32)
    slab = lax.axis_index("slab").astype(jnp.int32)
    core = slab & 1
    place_one = place[None]
    core_one = core[None]
    inverse = slab_inverse[0]
    column = inverse.reshape(2 * n, n)
    green = green_prev[0, 0]

    pieces = []
    for distance in range(energies):
        piece = lax.dynamic_slice_in_dim(green, (place ^ distance) * rows, rows, axis=1)
        pieces.append(piece if distance == 0 else exchange(piece, "energy", distance))

    partner = exchange(column, "slab", 1)
    low = jnp.where(core == 0, column, partner)
    high = jnp.where(core == 0, partner, column)
    right = jnp.concatenate(
        (
            jnp.concatenate((inverse[0], inverse[1]), axis=1),
            jnp.concatenate((-inverse[1], inverse[0]), axis=1),
        ),
        axis=0,
    )
    own_embed = jnp.concatenate(
        (
            jnp.concatenate((inverse[0], -inverse[1]), axis=1),
            jnp.concatenate((inverse[1], inverse[0]), axis=1),
        ),
        axis=0,
    )
    low_col, high_embed, own_factor = own_matrices(core_one, low, high, column, coupling_block)
    far = []
    chain = low_col
    for back in range(2, slabs, 2):
        far_self = shift(column, "slab", back)
        far_partner = exchange(far_self, "slab", 1)
        far_high = jnp.where(core == 0, far_partner, far_self)
        far.append(far_matrices(core_one, chain, far_high, far_self, coupling_block, high_embed))
        if back + 2 < slabs:
            far_low = jnp.where(core == 0, far_self, far_partner)
            for block in (far_high, far_low):
                step = jnp.dot(block, coupling_block, preferred_element_type=F32).astype(BF16)
                real, imag = chain[:n], chain[n:]
                chain = jnp.concatenate(
                    (
                        jnp.dot(real, step[:n], preferred_element_type=F32)
                        - jnp.dot(imag, step[n:], preferred_element_type=F32),
                        jnp.dot(real, step[n:], preferred_element_type=F32)
                        + jnp.dot(imag, step[:n], preferred_element_type=F32),
                    ),
                    axis=0,
                ).astype(BF16)

    mixed = mix(place_one, pair_source, pair_mode, phonon_coupling, pieces)
    back = [mixed[0]] + [exchange(mixed[d], "energy", d) for d in range(1, energies)]

    mask = (slab < active_slabs).astype(F32)
    scalars = jnp.concatenate((mask, offset))
    groups = [(0, energies // 2), (energies // 2, 3 * energies // 4), (3 * energies // 4, energies)]
    bases, own_chunks = [], []
    for first, last in groups:
        count = last - first
        base = (place ^ first) // count
        bases.append(base)
        own_chunks.append(
            right_rows(jnp.stack((base, place ^ first)), scalars, right, inverse, back[first:last])
        )
    bases = jnp.stack(bases)
    far_chunks = [
        [shift(chunk, "slab", 2 * (index + 1)) for chunk in own_chunks] for index in range(len(far))
    ]
    to_partner = left_sum(
        bases,
        [(own_chunks, high_embed, own_factor, None)]
        + [(chunks, moves, factors, 1) for chunks, (moves, factors) in zip(far_chunks, far)],
        BF16,
        n,
    )
    from_partner = exchange(to_partner, "slab", 1)
    own_sum = left_sum(
        bases,
        [(own_chunks, None, own_embed, None)]
        + [(chunks, moves, factors, 0) for chunks, (moves, factors) in zip(far_chunks, far)],
        F32,
        n,
    )
    current, terms = finish(occupation, own_sum, from_partner)
    spread = jnp.broadcast_to(terms[None], (energies, 1, n))
    density = jnp.sum(lax.all_to_all(spread, "energy", 0, 0, tiled=True), axis=0)
    return (current.reshape(1, 1, 2, n, n), density)


def solution(mesh):
    in_specs = (
        P("energy", "slab", None, None, None),
        P("slab", None, None, None),
        P(),
        P(None, "energy", None),
        P("energy"),
        P("energy"),
        P(),
        P(),
        P("energy"),
    )
    out_specs = (P("energy", "slab", None, None, None), P("slab", None))
    return jax.shard_map(local, mesh=mesh, in_specs=in_specs, out_specs=out_specs, check_vma=False)
```

```python
import functools

import jax
import jax.numpy as jnp
from jax import lax
from jax.experimental import pallas as pl
from jax.experimental.pallas import tpu as pltpu
from jax.sharding import PartitionSpec as P

BF16 = jnp.bfloat16
F32 = jnp.float32
VMEM = pl.BlockSpec(memory_space=pltpu.VMEM)
SMEM = pl.BlockSpec(memory_space=pltpu.SMEM)


def mxu(first, second):
    return jnp.dot(first, second, preferred_element_type=F32)


def mxu_nt(first, second):
    return lax.dot_general(first, second, (((1,), (1,)), ((), ())), preferred_element_type=F32)


def call(kernel, out_shape, in_specs, scratch=(), out_specs=None, flops=0, bytes_accessed=0, vmem=16):
    return pl.pallas_call(
        kernel,
        out_shape=out_shape,
        in_specs=in_specs,
        out_specs=jax.tree.map(lambda _: VMEM, out_shape) if out_specs is None else out_specs,
        scratch_shapes=list(scratch),
        compiler_params=pltpu.CompilerParams(vmem_limit_bytes=vmem * 2**20),
        cost_estimate=pl.CostEstimate(flops=flops, bytes_accessed=bytes_accessed, transcendentals=0),
    )


def complex_of(by_real, by_imag):
    rows = by_real.shape[0] // 2
    return by_real[:rows] - by_imag[rows:], by_real[rows:] + by_imag[:rows]


def product(first, second):
    rows = second.shape[0] // 2
    return complex_of(mxu(first, second[:rows]), mxu(first, second[rows:]))


def store(ref, parts):
    rows = parts[0].shape[0]
    for index, part in enumerate(parts):
        ref[index * rows : (index + 1) * rows, :] = part.astype(ref.dtype)


def mix_kernel(place_ref, source_ref, mode_ref, phonon_ref, *refs):
    energies = (len(refs) - 2) // 2
    pieces, outs = refs[:energies], refs[energies : 2 * energies]
    green, phonon = refs[2 * energies :]
    place = place_ref[0]
    pairs = source_ref.shape[1]
    rows, n = phonon_ref.shape[1:]
    phonon[...] = phonon_ref[...].astype(F32)
    for distance in range(energies):
        green[distance] = pieces[distance][...].astype(F32)
    step = 16

    @pl.loop(0, rows // step)
    def _(block):
        at = pl.ds(pl.multiple_of(block * step, step), step)
        for distance in range(energies):
            energy = place ^ distance
            real = jnp.zeros((step, n), F32)
            imag = jnp.zeros((step, n), F32)
            for pair in range(pairs):
                origin = source_ref[energy, pair] ^ place
                factor = phonon[mode_ref[energy, pair], at, :]
                real = real + factor * green[origin, 0, at, :]
                imag = imag + factor * green[origin, 1, at, :]
            outs[distance][0, at, :] = real.astype(BF16)
            outs[distance][1, at, :] = imag.astype(BF16)


def mix(place, source, mode, phonon, pieces):
    energies = len(pieces)
    _, rows, n = pieces[0].shape
    return call(
        mix_kernel,
        [jax.ShapeDtypeStruct((2, rows, n), BF16)] * energies,
        [SMEM] * 3 + [VMEM] * (energies + 1),
        [pltpu.VMEM((energies, 2, rows, n), F32), pltpu.VMEM(phonon.shape, F32)],
        flops=energies * 24 * rows * n * 16,
        bytes_accessed=energies * rows * n * 8,
        vmem=12,
    )(place, source, mode, phonon, *pieces)


def right_kernel(place_ref, slab_ref, active_ref, offset_ref, inverse_ref, *refs, first):
    pieces, out_ref, rows_ref = refs[:-2], refs[-2], refs[-1]
    count = len(pieces)
    place = place_ref[0] ^ first
    rows, n = pieces[0].shape[1:]
    total = count * rows
    for index, piece in enumerate(pieces):
        at = (place ^ index) & (count - 1)
        for part in range(2):
            rows_ref[pl.ds(pl.multiple_of(part * total + at * rows, rows), rows), :] = piece[part]
    mask = jnp.where(slab_ref[0] < active_ref[0], 1.0, 0.0)
    offset = offset_ref[0]
    start = pl.multiple_of(place // count * total, total)
    eye = (
        lax.broadcasted_iota(jnp.int32, (total, n), 0) + start
        == lax.broadcasted_iota(jnp.int32, (total, n), 1)
    ).astype(F32)
    real, imag = product(rows_ref[...], inverse_ref[...])
    own_real = inverse_ref[pl.ds(start, total), :].astype(F32)
    own_imag = inverse_ref[pl.ds(pl.multiple_of(n + start, total), total), :].astype(F32)
    store(out_ref, (mask * real + offset * own_real + eye, mask * imag + offset * own_imag))


def right_rows(scalars, inverse, pieces, first):
    _, rows, n = pieces[0].shape
    total = rows * len(pieces)
    return call(
        functools.partial(right_kernel, first=first),
        jax.ShapeDtypeStruct((2 * total, n), BF16),
        [SMEM] * 4 + [VMEM] * (1 + len(pieces)),
        [pltpu.VMEM((2 * total, n), BF16)],
        flops=8 * total * n * n,
        bytes_accessed=8 * n * n,
        vmem=12,
    )(*scalars, inverse, *pieces)


def own_matrices_kernel(slab_ref, self_ref, partner_ref, coupling_ref, low_ref, high_ref, factor_ref, both):
    core = slab_ref[0] & 1
    both[core] = self_ref[...]
    both[1 - core] = partner_ref[...]
    coupling = coupling_ref[...]
    low_ref[...] = mxu(both[0], coupling).astype(BF16)
    high_ref[...] = mxu(both[1], coupling).astype(BF16)

    @pl.when(core == 0)
    def _():
        store(factor_ref, product(high_ref[...], self_ref[...]))

    @pl.when(core != 0)
    def _():
        factor_ref[...] = jnp.zeros_like(factor_ref)


def own_matrices(slab, own, partner, coupling):
    n = coupling.shape[0]
    matrix = jax.ShapeDtypeStruct((2 * n, n), BF16)
    return call(
        own_matrices_kernel,
        [matrix, matrix, matrix],
        [SMEM] + [VMEM] * 3,
        [pltpu.VMEM((2, 2 * n, n), BF16)],
        flops=16 * n**3,
        bytes_accessed=14 * n * n,
        vmem=20,
    )(slab, own, partner, coupling)


def far_matrices_kernel(slab_ref, chain_ref, self_ref, partner_ref, coupling_ref, high_ref, moves, factors):
    core = slab_ref[0] & 1
    low, high = core, 1 - core

    @pl.when(core == 0)
    def _():
        far_high = mxu(partner_ref[...], coupling_ref[...]).astype(BF16)
        store(moves.at[low], product(chain_ref[...], far_high))

    @pl.when(core != 0)
    def _():
        moves[low] = chain_ref[...]

    store(moves.at[high], product(high_ref[...], moves[low]))
    for place in range(2):
        store(factors.at[place], product(moves[place], self_ref[...]))


def far_matrices(slab, chain, far_self, far_partner, coupling, high):
    n = coupling.shape[0]
    pair = jax.ShapeDtypeStruct((2, 2 * n, n), BF16)
    return call(
        far_matrices_kernel,
        [pair, pair],
        [SMEM] + [VMEM] * 5,
        flops=36 * n**3,
        bytes_accessed=20 * n * n,
        vmem=20,
    )(slab, chain, far_self, far_partner, coupling, high)


def block_of(place, first, size, n, energies):
    return (place ^ first) // (size * energies // n)


def moved_term(rows, move, factor):
    n = move.shape[0] // 2
    moved = complex_of(mxu_nt(rows, move[:n]), mxu_nt(rows, move[n:]))
    moved = [part.astype(BF16) for part in moved]
    return complex_of(mxu(factor, moved[0]), mxu(factor, moved[1]))


def own_terms_kernel(place_ref, high_ref, own_ref, factor_ref, *refs, firsts, energies):
    chunks, (self_ref, partner_ref, rows_ref) = refs[:-3], refs[-3:]
    n = self_ref.shape[1]
    for index, chunk in enumerate(chunks):
        size = chunk.shape[0] // 2
        for part in range(2):
            start = pl.multiple_of(part * n + block_of(place_ref[0], firsts[index], size, n, energies) * size, size)
            rows_ref[pl.ds(start, size), :] = chunk[part * size : (part + 1) * size, :]
    store(partner_ref, moved_term(rows_ref[...], high_ref[...], factor_ref[...]))
    store(self_ref, product(own_ref[...], rows_ref[...]))


def own_terms(place, high, own, factor, chunks, firsts, energies):
    n = own.shape[1]
    total = jax.ShapeDtypeStruct((2 * n, n), F32)
    return call(
        functools.partial(own_terms_kernel, firsts=tuple(firsts), energies=energies),
        [total, total],
        [SMEM] + [VMEM] * (3 + len(chunks)),
        [pltpu.VMEM((2 * n, n), BF16)],
        flops=24 * n**3,
        bytes_accessed=28 * n * n,
        vmem=20,
    )(place, high, own, factor, *chunks)


def far_terms_kernel(place_ref, total_ref, *refs, target, firsts, energies):
    count = len(firsts)
    out_ref, refs = refs[-1], refs[:-1]
    n = total_ref.shape[1]
    total = [total_ref[:n, :], total_ref[n:, :]]
    for term in range(len(refs) // (count + 2)):
        group = refs[term * (count + 2) : (term + 1) * (count + 2)]
        moves, factors = group[count].at[target], group[count + 1].at[target]
        for index in range(count):
            block = group[index]
            size = block.shape[0] // 2
            start = pl.multiple_of(block_of(place_ref[0], firsts[index], size, n, energies) * size, size)
            parts = moved_term(block[...], moves[...], factors[:, pl.ds(start, size)])
            total = [a + b for a, b in zip(total, parts)]
    store(out_ref, total)


def far_terms(place, total, terms, firsts, target, dtype, energies):
    n = total.shape[1]
    arrays = [array for chunks, moves, factors in terms for array in (*chunks, moves, factors)]
    rows = sum(chunk.shape[0] // 2 for chunk in terms[0][0])
    return call(
        functools.partial(far_terms_kernel, target=target, firsts=tuple(firsts), energies=energies),
        jax.ShapeDtypeStruct((2 * n, n), dtype),
        [SMEM] + [VMEM] * (1 + len(arrays)),
        flops=16 * n**2 * rows * len(terms),
        bytes_accessed=16 * n * n * len(terms),
        vmem=20 + 5 * (len(terms) - 1),
    )(place, total, *arrays)


def finish_kernel(scalar_ref, own_ref, partner_ref, green_ref, density_ref):
    n = own_ref.shape[1]
    green = (own_ref[...] + partner_ref[...].astype(F32)).astype(BF16)
    green_ref[...] = green
    eye = lax.broadcasted_iota(jnp.int32, (n, n), 0) == lax.broadcasted_iota(jnp.int32, (n, n), 1)
    diagonal = jnp.sum(jnp.where(eye, green[n:].astype(F32), 0.0), axis=0, keepdims=True)
    density_ref[...] = -scalar_ref[0] * diagonal


def finish(scalars, own, partner):
    n = own.shape[1]
    return call(
        finish_kernel,
        [jax.ShapeDtypeStruct((2 * n, n), BF16), jax.ShapeDtypeStruct((1, n), F32)],
        [SMEM, VMEM, VMEM],
        flops=8 * n * n,
        bytes_accessed=16 * n * n,
    )(scalars, own, partner)


def exchange(x, axis, distance):
    size = lax.axis_size(axis)
    return lax.ppermute(x, axis, [(i, i ^ distance) for i in range(size)])


def shift(x, axis, by):
    size = lax.axis_size(axis)
    return lax.ppermute(x, axis, [(i, i + by) for i in range(size - by)])


def after(x, *others):
    return lax.optimization_barrier((x, *others))[0]


def exchange_all(pieces, window):
    received = [pieces[0]]
    for distance in range(1, len(pieces)):
        piece = pieces[distance]
        if distance > window:
            piece = after(piece, received[distance - window])
        received.append(exchange(piece, "energy", distance))
    return received


def complex_columns(first, second, n):
    real, imag = first[:n], first[n:]
    dot = functools.partial(jnp.dot, preferred_element_type=F32)
    return jnp.concatenate(
        (
            dot(real, second[:n]) - dot(imag, second[n:]),
            dot(real, second[n:]) + dot(imag, second[:n]),
        ),
        axis=0,
    ).astype(BF16)


def local(
    green_prev,
    slab_inverse,
    coupling_block,
    phonon_coupling,
    offset,
    occupation,
    pair_source,
    pair_mode,
    active_slabs,
):
    energies = pair_source.shape[0]
    n = coupling_block.shape[0]
    rows = n // energies
    slabs = lax.axis_size("slab")
    place = lax.axis_index("energy").astype(jnp.int32)
    slab = lax.axis_index("slab").astype(jnp.int32)
    core = slab & 1
    place_one = place[None]
    slab_one = slab[None]
    column = slab_inverse[0].reshape(2 * n, n)
    green = green_prev[0, 0]

    sent = [
        lax.dynamic_slice_in_dim(green, (place ^ distance) * rows, rows, axis=1)
        for distance in range(energies)
    ]
    pieces = exchange_all(sent, 4)

    partner = exchange(column, "slab", 1)
    low_move, high_move, own_factor = own_matrices(slab_one, column, partner, coupling_block)
    far_selves = [shift(column, "slab", back) for back in range(2, slabs, 2)]

    pieces[-1] = after(pieces[-1], high_move)
    mixed = mix(place_one, pair_source, pair_mode, phonon_coupling, pieces)
    back = exchange_all(mixed, 4)

    far_blocks = []
    for far_self in far_selves:
        far_self = after(far_self, mixed[1])
        far_blocks.append((far_self, exchange(far_self, "slab", 1)))
    far = []
    chain = after(low_move, back[2])
    for far_self, far_partner in far_blocks:
        if far:
            far_self_old, far_partner_old = far_blocks[len(far) - 1]
            high = jnp.where(core == 0, far_partner_old, far_self_old)
            low = jnp.where(core == 0, far_self_old, far_partner_old)
            for block in (high, low):
                step = jnp.dot(block, coupling_block, preferred_element_type=F32).astype(BF16)
                chain = complex_columns(chain, step, n)
        far.append(far_matrices(slab_one, chain, far_self, far_partner, coupling_block, high_move))

    scalars = (place_one, slab_one, active_slabs, offset)
    groups = [(0, energies // 2), (energies // 2, 3 * energies // 4), (3 * energies // 4, energies)]
    firsts = [first for first, _ in groups]
    if far:
        back[-1] = after(back[-1], far[-1][0])
    own_chunks = [right_rows(scalars, column, back[first:last], first) for first, last in groups]
    far_chunks = [
        [shift(chunk, "slab", 2 * (index + 1)) for chunk in own_chunks] for index in range(len(far))
    ]
    for_self, for_partner = own_terms(place_one, high_move, column, own_factor, own_chunks, firsts, energies)
    for first, last in ((0, 1), (1, 3)):
        terms = [(chunks[first:last], *matrices) for chunks, matrices in zip(far_chunks, far)]
        if terms:
            far_of = functools.partial(far_terms, place_one, terms=terms, firsts=firsts[first:last], energies=energies)
            for_partner = far_of(total=for_partner, target=1, dtype=F32 if first == 0 else BF16)
            for_self = far_of(total=for_self, target=0, dtype=F32)
    from_partner = exchange(for_partner.astype(BF16), "slab", 1)
    current, terms = finish(occupation, for_self, from_partner)
    spread = jnp.broadcast_to(terms[None], (energies, 1, n))
    density = jnp.sum(lax.all_to_all(spread, "energy", 0, 0, tiled=True), axis=0)
    return (current.reshape(1, 1, 2, n, n), density)


def solution(mesh):
    in_specs = (
        P("energy", "slab", None, None, None),
        P("slab", None, None, None),
        P(),
        P(None, "energy", None),
        P("energy"),
        P("energy"),
        P(),
        P(),
        P("energy"),
    )
    out_specs = (P("energy", "slab", None, None, None), P("slab", None))
    return jax.shard_map(local, mesh=mesh, in_specs=in_specs, out_specs=out_specs, check_vma=False)
```

```python
import functools

import jax
import jax.numpy as jnp
from jax import lax
from jax.experimental import pallas as pl
from jax.experimental.pallas import tpu as pltpu
from jax.sharding import PartitionSpec as P

BF16 = jnp.bfloat16
F32 = jnp.float32
MICROSECOND = 3_300_000
VMEM = pl.BlockSpec(memory_space=pltpu.VMEM)
SMEM = pl.BlockSpec(memory_space=pltpu.SMEM)


def mxu(first, second):
    return jnp.dot(first, second, preferred_element_type=F32)


def mxu_nt(first, second):
    return lax.dot_general(first, second, (((1,), (1,)), ((), ())), preferred_element_type=F32)


def call(kernel, out_shape, in_specs, scratch=(), vmem=16, cost=0.0):
    return pl.pallas_call(
        kernel,
        out_shape=out_shape,
        in_specs=in_specs,
        out_specs=jax.tree.map(lambda _: VMEM, out_shape),
        scratch_shapes=list(scratch),
        compiler_params=pltpu.CompilerParams(vmem_limit_bytes=vmem * 2**20),
        cost_estimate=pl.CostEstimate(
            flops=1024, bytes_accessed=1024 + int(cost * MICROSECOND), transcendentals=0
        ),
    )


def complex_of(by_real, by_imag):
    rows = by_real.shape[0] // 2
    return by_real[:rows] - by_imag[rows:], by_real[rows:] + by_imag[:rows]


def product(first, second):
    rows = second.shape[0] // 2
    return complex_of(mxu(first, second[:rows]), mxu(first, second[rows:]))


def store(ref, parts):
    rows = parts[0].shape[0]
    for index, part in enumerate(parts):
        ref[index * rows : (index + 1) * rows, :] = part.astype(ref.dtype)


def mix_kernel(place_ref, source_ref, mode_ref, phonon_ref, *refs):
    energies = (len(refs) - 2) // 2
    pieces, outs = refs[:energies], refs[energies : 2 * energies]
    green, phonon = refs[2 * energies :]
    place = place_ref[0]
    pairs = source_ref.shape[1]
    rows, n = phonon_ref.shape[1:]
    phonon[...] = phonon_ref[...].astype(F32)
    for distance in range(energies):
        green[place ^ distance] = pieces[distance][...].astype(F32)
    step = 16

    @pl.loop(0, rows // step)
    def _(block):
        at = pl.ds(pl.multiple_of(block * step, step), step)
        for distance in range(energies):
            energy = place ^ distance
            real = jnp.zeros((step, n), F32)
            imag = jnp.zeros((step, n), F32)
            for pair in range(pairs):
                origin = source_ref[energy, pair]
                factor = phonon[mode_ref[energy, pair], at, :]
                real = real + factor * green[origin, 0, at, :]
                imag = imag + factor * green[origin, 1, at, :]
            outs[distance][0, at, :] = real.astype(BF16)
            outs[distance][1, at, :] = imag.astype(BF16)


def mix(place, source, mode, phonon, pieces):
    energies = len(pieces)
    _, rows, n = pieces[0].shape
    return call(
        mix_kernel,
        [jax.ShapeDtypeStruct((2, rows, n), BF16)] * energies,
        [SMEM] * 3 + [VMEM] * (energies + 1),
        [pltpu.VMEM((energies, 2, rows, n), F32), pltpu.VMEM(phonon.shape, F32)],
        vmem=12,
        cost=2.0,
    )(place, source, mode, phonon, *pieces)


def arrived_kernel(*refs):
    refs[-1][...] = jnp.zeros_like(refs[-1])


def arrived(*arrays):
    anywhere = pl.BlockSpec(memory_space=pl.ANY)
    return call(
        arrived_kernel, jax.ShapeDtypeStruct((8, 128), F32), [anywhere] * len(arrays), vmem=1, cost=60.0
    )(*arrays)


def right_kernel(place_ref, slab_ref, active_ref, offset_ref, inverse_ref, *refs, first):
    pieces, out_ref, rows_ref = refs[:-2], refs[-2], refs[-1]
    count = len(pieces)
    place = place_ref[0] ^ first
    rows, n = pieces[0].shape[1:]
    total = count * rows
    for index, piece in enumerate(pieces):
        at = (place ^ index) & (count - 1)
        for part in range(2):
            rows_ref[pl.ds(pl.multiple_of(part * total + at * rows, rows), rows), :] = piece[part]
    mask = jnp.where(slab_ref[0] < active_ref[0], 1.0, 0.0)
    offset = offset_ref[0]
    start = pl.multiple_of(place // count * total, total)
    eye = (
        lax.broadcasted_iota(jnp.int32, (total, n), 0) + start
        == lax.broadcasted_iota(jnp.int32, (total, n), 1)
    ).astype(F32)
    real, imag = product(rows_ref[...], inverse_ref[...])
    own_real = inverse_ref[pl.ds(start, total), :].astype(F32)
    own_imag = inverse_ref[pl.ds(pl.multiple_of(n + start, total), total), :].astype(F32)
    store(out_ref, (mask * real + offset * own_real + eye, mask * imag + offset * own_imag))


def right_rows(scalars, inverse, pieces, first, cost=0.8):
    _, rows, n = pieces[0].shape
    total = rows * len(pieces)
    return call(
        functools.partial(right_kernel, first=first),
        jax.ShapeDtypeStruct((2 * total, n), BF16),
        [SMEM] * 4 + [VMEM] * (1 + len(pieces)),
        [pltpu.VMEM((2 * total, n), BF16)],
        vmem=12,
        cost=cost,
    )(*scalars, inverse, *pieces)


def own_matrices_kernel(slab_ref, self_ref, partner_ref, coupling_ref, low_ref, high_ref, factor_ref, both):
    core = slab_ref[0] & 1
    both[core] = self_ref[...]
    both[1 - core] = partner_ref[...]
    coupling = coupling_ref[...]
    low_ref[...] = mxu(both[0], coupling).astype(BF16)
    high_ref[...] = mxu(both[1], coupling).astype(BF16)

    @pl.when(core == 0)
    def _():
        store(factor_ref, product(high_ref[...], self_ref[...]))

    @pl.when(core != 0)
    def _():
        factor_ref[...] = jnp.zeros_like(factor_ref)


def own_matrices(slab, own, partner, coupling):
    n = coupling.shape[0]
    matrix = jax.ShapeDtypeStruct((2 * n, n), BF16)
    return call(
        own_matrices_kernel,
        [matrix, matrix, matrix],
        [SMEM] + [VMEM] * 3,
        [pltpu.VMEM((2, 2 * n, n), BF16)],
        vmem=20,
        cost=3.0,
    )(slab, own, partner, coupling)


def far_matrices_kernel(slab_ref, chain_ref, self_ref, partner_ref, coupling_ref, high_ref, moves, factors, *more):
    core = slab_ref[0] & 1
    low, high = core, 1 - core

    def chain_and_high(high_inverse):
        step = mxu(high_inverse, coupling_ref[...]).astype(BF16)
        store(moves.at[high], product(chain_ref[...], step))

    @pl.when(core == 0)
    def _():
        chain_and_high(partner_ref[...])
        moves[low] = moves[high]
        for chain in more:
            step = mxu(self_ref[...], coupling_ref[...]).astype(BF16)
            store(chain, product(moves[high], step))

    @pl.when(core != 0)
    def _():
        moves[low] = chain_ref[...]
        for chain in more:
            chain_and_high(self_ref[...])
            step = mxu(partner_ref[...], coupling_ref[...]).astype(BF16)
            store(chain, product(moves[high], step))

    store(moves.at[high], product(high_ref[...], moves[low]))
    for place in range(2):
        store(factors.at[place], product(moves[place], self_ref[...]))


def far_matrices(slab, chain, far_self, far_partner, coupling, high, goes_on):
    n = coupling.shape[0]
    matrix = jax.ShapeDtypeStruct((2 * n, n), BF16)
    pair = jax.ShapeDtypeStruct((2, 2 * n, n), BF16)
    return call(
        far_matrices_kernel,
        [pair, pair] + [matrix] * goes_on,
        [SMEM] + [VMEM] * 5,
        vmem=24,
        cost=5.2,
    )(slab, chain, far_self, far_partner, coupling, high)


def block_of(place, first, size, n, energies):
    return (place ^ first) // (size * energies // n)


def moved_term(rows, move, factor):
    n = move.shape[0] // 2
    moved = complex_of(mxu_nt(rows, move[:n]), mxu_nt(rows, move[n:]))
    moved = [part.astype(BF16) for part in moved]
    return complex_of(mxu(factor, moved[0]), mxu(factor, moved[1]))


def own_terms_kernel(place_ref, high_ref, own_ref, factor_ref, *refs, firsts, energies):
    chunks, (self_ref, partner_ref, rows_ref) = refs[:-3], refs[-3:]
    n = self_ref.shape[1]
    for index, chunk in enumerate(chunks):
        size = chunk.shape[0] // 2
        for part in range(2):
            start = pl.multiple_of(part * n + block_of(place_ref[0], firsts[index], size, n, energies) * size, size)
            rows_ref[pl.ds(start, size), :] = chunk[part * size : (part + 1) * size, :]
    store(partner_ref, moved_term(rows_ref[...], high_ref[...], factor_ref[...]))
    store(self_ref, product(own_ref[...], rows_ref[...]))


def own_terms(place, high, own, factor, chunks, firsts, energies):
    n = own.shape[1]
    total = jax.ShapeDtypeStruct((2 * n, n), F32)
    return call(
        functools.partial(own_terms_kernel, firsts=tuple(firsts), energies=energies),
        [total, total],
        [SMEM] + [VMEM] * (3 + len(chunks)),
        [pltpu.VMEM((2 * n, n), BF16)],
        vmem=20,
        cost=3.6,
    )(place, high, own, factor, *chunks)


def far_terms_kernel(place_ref, total_ref, *refs, target, firsts, energies):
    count = len(firsts)
    out_ref, refs = refs[-1], refs[:-1]
    n = total_ref.shape[1]
    total = [total_ref[:n, :], total_ref[n:, :]]
    for term in range(len(refs) // (count + 2)):
        group = refs[term * (count + 2) : (term + 1) * (count + 2)]
        moves, factors = group[count].at[target], group[count + 1].at[target]
        for index in range(count):
            block = group[index]
            size = block.shape[0] // 2
            start = pl.multiple_of(block_of(place_ref[0], firsts[index], size, n, energies) * size, size)
            parts = moved_term(block[...], moves[...], factors[:, pl.ds(start, size)])
            total = [a + b for a, b in zip(total, parts)]
    store(out_ref, total)


def far_terms(place, total, terms, firsts, target, dtype, energies):
    n = total.shape[1]
    arrays = [array for chunks, moves, factors in terms for array in (*chunks, moves, factors)]
    rows = sum(chunk.shape[0] // 2 for chunk in terms[0][0])
    return call(
        functools.partial(far_terms_kernel, target=target, firsts=tuple(firsts), energies=energies),
        jax.ShapeDtypeStruct((2 * n, n), dtype),
        [SMEM] + [VMEM] * (1 + len(arrays)),
        vmem=20 + 5 * (len(terms) - 1),
        cost=1.8,
    )(place, total, *arrays)


def finish_kernel(scalar_ref, own_ref, partner_ref, green_ref, density_ref):
    n = own_ref.shape[1]
    green = (own_ref[...] + partner_ref[...].astype(F32)).astype(BF16)
    green_ref[...] = green
    eye = lax.broadcasted_iota(jnp.int32, (n, n), 0) == lax.broadcasted_iota(jnp.int32, (n, n), 1)
    diagonal = jnp.sum(jnp.where(eye, green[n:].astype(F32), 0.0), axis=0, keepdims=True)
    density_ref[...] = -scalar_ref[0] * diagonal


def finish(scalars, own, partner):
    n = own.shape[1]
    return call(
        finish_kernel,
        [jax.ShapeDtypeStruct((2 * n, n), BF16), jax.ShapeDtypeStruct((1, n), F32)],
        [SMEM, VMEM, VMEM],
    )(scalars, own, partner)


def exchange(x, axis, distance):
    size = lax.axis_size(axis)
    return lax.ppermute(x, axis, [(i, i ^ distance) for i in range(size)])


def shift(x, axis, by):
    size = lax.axis_size(axis)
    return lax.ppermute(x, axis, [(i, i + by) for i in range(size - by)])


def after(x, *others):
    return lax.optimization_barrier((x, *others))[0]


def exchange_all(pieces, order, window):
    received = list(pieces)
    for at, distance in enumerate(order):
        piece = pieces[distance]
        if at >= window:
            piece = after(piece, received[order[at - window]])
        received[distance] = exchange(piece, "energy", distance)
    return received


def local(
    green_prev,
    slab_inverse,
    coupling_block,
    phonon_coupling,
    offset,
    occupation,
    pair_source,
    pair_mode,
    active_slabs,
):
    energies = pair_source.shape[0]
    n = coupling_block.shape[0]
    rows = n // energies
    slabs = lax.axis_size("slab")
    place = lax.axis_index("energy").astype(jnp.int32)
    slab = lax.axis_index("slab").astype(jnp.int32)
    core = slab & 1
    place_one = place[None]
    slab_one = slab[None]
    column = slab_inverse[0].reshape(2 * n, n)
    green = green_prev[0, 0]

    half = energies // 2
    partner = exchange(column, "slab", 1)
    far_selves = [shift(column, "slab", behind) for behind in range(2, slabs, 2)]
    sent = [
        lax.dynamic_slice_in_dim(green, (place ^ distance) * rows, rows, axis=1)
        for distance in range(energies)
    ]
    sent[1] = after(sent[1], partner)
    pieces = exchange_all(sent, range(1, energies), energies)
    mixed = mix(place_one, pair_source, pair_mode, phonon_coupling, pieces)
    far_partners = [exchange(after(far_self, mixed[1]), "slab", 1) for far_self in far_selves]
    back = exchange_all(mixed, range(1, energies), energies)
    back[1] = after(back[1], *far_partners)

    scalars = (place_one, slab_one, active_slabs, offset)
    groups = [(0, half), (half, energies)]
    firsts = [first for first, _ in groups]
    own_chunks = [right_rows(scalars, column, back[:half], 0)]

    chain, high_move, own_factor = own_matrices(
        slab_one, column, after(partner, own_chunks[0]), coupling_block
    )
    far = []
    for index, (far_self, far_partner) in enumerate(zip(far_selves, far_partners)):
        moves, factors, *chain = far_matrices(
            slab_one,
            chain if index == 0 else chain[0],
            far_self,
            far_partner,
            coupling_block,
            high_move,
            index + 1 < len(far_selves),
        )
        far.append((moves, factors))
    if far:
        back[half] = after(back[half], far[-1][0])
    own_chunks += [right_rows(scalars, column, back[first:last], first, 30.0) for first, last in groups[1:]]
    far_chunks = [
        [shift(chunk, "slab", 2 * (index + 1)) for chunk in own_chunks] for index in range(len(far))
    ]
    for_self, for_partner = own_terms(place_one, high_move, column, own_factor, own_chunks, firsts, energies)
    for first, last in ((0, 1), (1, 2)):
        terms = [(chunks[first:last], *matrices) for chunks, matrices in zip(far_chunks, far)]
        if terms:
            if first > 0:
                terms[-1][0][-1] = after(terms[-1][0][-1], for_self, for_partner)
            far_of = functools.partial(far_terms, place_one, firsts=firsts[first:last], energies=energies)
            for_partner = far_of(terms=terms, total=for_partner, target=1, dtype=F32 if first == 0 else BF16)
            for_self = far_of(terms=terms, total=for_self, target=0, dtype=F32)
    from_partner = exchange(for_partner.astype(BF16), "slab", 1)
    current, terms = finish(occupation, for_self, from_partner)
    spread = jnp.broadcast_to(terms[None], (energies, 1, n))
    density = jnp.sum(lax.all_to_all(spread, "energy", 0, 0, tiled=True), axis=0)
    return (current.reshape(1, 1, 2, n, n), density)


def solution(mesh):
    in_specs = (
        P("energy", "slab", None, None, None),
        P("slab", None, None, None),
        P(),
        P(None, "energy", None),
        P("energy"),
        P("energy"),
        P(),
        P(),
        P("energy"),
    )
    out_specs = (P("energy", "slab", None, None, None), P("slab", None))
    return jax.shard_map(local, mesh=mesh, in_specs=in_specs, out_specs=out_specs, check_vma=False)
```

```python
import functools

import jax
import jax.numpy as jnp
from jax import lax
from jax.experimental import pallas as pl
from jax.experimental.pallas import tpu as pltpu
from jax.sharding import PartitionSpec as P

BF16 = jnp.bfloat16
F32 = jnp.float32
LANES = 128
MICROSECOND = 3_300_000
VMEM = pl.BlockSpec(memory_space=pltpu.VMEM)
SMEM = pl.BlockSpec(memory_space=pltpu.SMEM)


def mxu(first, second):
    return jnp.dot(first, second, preferred_element_type=F32)


def mxu_nt(first, second):
    return lax.dot_general(first, second, (((1,), (1,)), ((), ())), preferred_element_type=F32)


def call(kernel, out_shape, in_specs, scratch=(), vmem=16, cost=0.0):
    return pl.pallas_call(
        kernel,
        out_shape=out_shape,
        in_specs=in_specs,
        out_specs=jax.tree.map(lambda _: VMEM, out_shape),
        scratch_shapes=list(scratch),
        compiler_params=pltpu.CompilerParams(vmem_limit_bytes=vmem * 2**20),
        cost_estimate=pl.CostEstimate(
            flops=1024, bytes_accessed=1024 + int(cost * MICROSECOND), transcendentals=0
        ),
    )


def complex_of(by_real, by_imag):
    rows = by_real.shape[0] // 2
    return by_real[:rows] - by_imag[rows:], by_real[rows:] + by_imag[:rows]


def product(first, second):
    rows = second.shape[0] // 2
    return complex_of(mxu(first, second[:rows]), mxu(first, second[rows:]))


def store(ref, parts):
    rows = parts[0].shape[0]
    for index, part in enumerate(parts):
        ref[index * rows : (index + 1) * rows, :] = part.astype(ref.dtype)


def weight_kernel(slab_ref, active_ref, occupation_ref, offset_ref, out_ref):
    shape = out_ref.shape
    row = lax.broadcasted_iota(jnp.int32, shape, 0)
    lane = lax.broadcasted_iota(jnp.int32, shape, 1)
    weight = occupation_ref[0]
    active = jnp.where(slab_ref[0] < active_ref[0], weight, 0.0)
    rest = jnp.where(lane < 2 * LANES, weight, weight * offset_ref[0])
    rest = jnp.where(lane < LANES, active, rest)
    out = jnp.zeros(shape, F32)
    for index in range(3):
        part = rest.astype(BF16).astype(F32)
        out = jnp.where(row == index, part, out)
        rest = rest - part
    out_ref[...] = out.astype(BF16)


def weight_rows(slab, active, occupation, offset, n):
    shape = jax.ShapeDtypeStruct((8, n), BF16)
    return call(weight_kernel, shape, [SMEM] * 4, vmem=4)(slab, active, occupation, offset)


def wide(row, n):
    return jnp.concatenate([row[:, :LANES]] * (n // LANES), axis=1)


def mix_kernel(place_ref, source_ref, mode_ref, phonon_ref, *refs):
    energies = (len(refs) - 5) // 2
    pieces, outs = refs[:energies], refs[energies : 2 * energies]
    weighted_ref, totals_ref, green, phonon, weights = refs[2 * energies :]
    place = place_ref[0]
    pairs = source_ref.shape[1]
    rows, n = phonon_ref.shape[1:]
    phonon[...] = phonon_ref[...].astype(F32)
    totals = jnp.zeros((1, n), F32)
    for distance in range(energies):
        piece = pieces[distance]
        for part in range(2):
            green[place ^ distance, part] = piece[part * rows : (part + 1) * rows, :].astype(F32)
        parts = piece[2 * rows :, :].astype(F32)
        row = parts[0:1] + parts[1:2] + parts[2:3]
        totals = totals + row
        weights[place ^ distance] = jnp.broadcast_to(wide(row, n), (8, n))
    totals_ref[...] = jnp.broadcast_to(totals, totals_ref.shape)
    step = 16

    @pl.loop(0, rows // step)
    def _(block):
        at = pl.ds(pl.multiple_of(block * step, step), step)
        weighted_real = jnp.zeros((step, n), F32)
        weighted_imag = jnp.zeros((step, n), F32)
        for distance in range(energies):
            energy = place ^ distance
            real = jnp.zeros((step, n), F32)
            imag = jnp.zeros((step, n), F32)
            for pair in range(pairs):
                origin = source_ref[energy, pair]
                factor = phonon[mode_ref[energy, pair], at, :]
                real = real + factor * green[origin, 0, at, :]
                imag = imag + factor * green[origin, 1, at, :]
            outs[distance][0, at, :] = real.astype(BF16)
            outs[distance][1, at, :] = imag.astype(BF16)
            weight = weights[energy, 0:1, :]
            weighted_real = weighted_real + weight * real
            weighted_imag = weighted_imag + weight * imag
        weighted_ref[0, at, :] = weighted_real.astype(BF16)
        weighted_ref[1, at, :] = weighted_imag.astype(BF16)


def mix(place, source, mode, phonon, pieces):
    energies = len(pieces)
    _, rows, n = phonon.shape
    block = jax.ShapeDtypeStruct((2, rows, n), BF16)
    return call(
        mix_kernel,
        [block] * (energies + 1) + [jax.ShapeDtypeStruct((8, n), F32)],
        [SMEM] * 3 + [VMEM] * (energies + 1),
        [
            pltpu.VMEM((energies, 2, rows, n), F32),
            pltpu.VMEM(phonon.shape, F32),
            pltpu.VMEM((energies, 8, n), F32),
        ],
        vmem=12,
        cost=2.0,
    )(place, source, mode, phonon, *pieces)


def finished_rows(sigma, inverse_ref, start, mask, offset, one):
    size, n = sigma.shape[0] // 2, sigma.shape[1]
    eye = (
        lax.broadcasted_iota(jnp.int32, (size, n), 0) + start
        == lax.broadcasted_iota(jnp.int32, (size, n), 1)
    ).astype(F32)
    real, imag = product(sigma, inverse_ref[...])
    own_real = inverse_ref[pl.ds(start, size), :].astype(F32)
    own_imag = inverse_ref[pl.ds(pl.multiple_of(n + start, size), size), :].astype(F32)
    return mask * real + offset * own_real + one * eye, mask * imag + offset * own_imag


def right_kernel(place_ref, slab_ref, active_ref, offset_ref, inverse_ref, *refs, first):
    pieces, out_ref, rows_ref = refs[:-2], refs[-2], refs[-1]
    count = len(pieces)
    place = place_ref[0] ^ first
    rows = pieces[0].shape[1]
    total = count * rows
    for index, piece in enumerate(pieces):
        at = (place ^ index) & (count - 1)
        for part in range(2):
            rows_ref[pl.ds(pl.multiple_of(part * total + at * rows, rows), rows), :] = piece[part]
    mask = jnp.where(slab_ref[0] < active_ref[0], 1.0, 0.0)
    start = pl.multiple_of(place // count * total, total)
    store(out_ref, finished_rows(rows_ref[...], inverse_ref, start, mask, offset_ref[0], 1.0))


def right_rows(scalars, inverse, pieces, first):
    _, rows, n = pieces[0].shape
    total = rows * len(pieces)
    return call(
        functools.partial(right_kernel, first=first),
        jax.ShapeDtypeStruct((2 * total, n), BF16),
        [SMEM] * 4 + [VMEM] * (1 + len(pieces)),
        [pltpu.VMEM((2 * total, n), BF16)],
        vmem=12,
        cost=0.8,
    )(*scalars, inverse, *pieces)


def weighted_kernel(place_ref, inverse_ref, sigma_ref, totals_ref, out_ref):
    _, rows, n = sigma_ref.shape
    start = pl.multiple_of(place_ref[0] * rows, rows)
    one = wide(totals_ref[0:1, LANES : 2 * LANES], n)
    offset = wide(totals_ref[0:1, 2 * LANES : 3 * LANES], n)
    sigma = sigma_ref[...].reshape(2 * rows, n)
    store(out_ref, finished_rows(sigma, inverse_ref, start, 1.0, offset, one))


def weighted_rows(place, inverse, sigma, totals):
    _, rows, n = sigma.shape
    return call(
        weighted_kernel,
        jax.ShapeDtypeStruct((2 * rows, n), BF16),
        [SMEM] + [VMEM] * 3,
        vmem=8,
        cost=0.3,
    )(place, inverse, sigma, totals)


def own_matrices_kernel(slab_ref, self_ref, partner_ref, coupling_ref, low_ref, high_ref, factor_ref, both):
    core = slab_ref[0] & 1
    both[core] = self_ref[...]
    both[1 - core] = partner_ref[...]
    coupling = coupling_ref[...]
    low_ref[...] = mxu(both[0], coupling).astype(BF16)
    high_ref[...] = mxu(both[1], coupling).astype(BF16)

    @pl.when(core == 0)
    def _():
        store(factor_ref, product(high_ref[...], self_ref[...]))

    @pl.when(core != 0)
    def _():
        factor_ref[...] = jnp.zeros_like(factor_ref)


def own_matrices(slab, own, partner, coupling):
    n = coupling.shape[0]
    matrix = jax.ShapeDtypeStruct((2 * n, n), BF16)
    return call(
        own_matrices_kernel,
        [matrix, matrix, matrix],
        [SMEM] + [VMEM] * 3,
        [pltpu.VMEM((2, 2 * n, n), BF16)],
        vmem=20,
        cost=0.0,
    )(slab, own, partner, coupling)


def far_matrices_kernel(slab_ref, chain_ref, self_ref, partner_ref, coupling_ref, high_ref, moves, factors, *more):
    core = slab_ref[0] & 1
    low, high = core, 1 - core

    def chain_and_high(high_inverse):
        step = mxu(high_inverse, coupling_ref[...]).astype(BF16)
        store(moves.at[high], product(chain_ref[...], step))

    @pl.when(core == 0)
    def _():
        chain_and_high(partner_ref[...])
        moves[low] = moves[high]
        for chain in more:
            step = mxu(self_ref[...], coupling_ref[...]).astype(BF16)
            store(chain, product(moves[high], step))

    @pl.when(core != 0)
    def _():
        moves[low] = chain_ref[...]
        for chain in more:
            chain_and_high(self_ref[...])
            step = mxu(partner_ref[...], coupling_ref[...]).astype(BF16)
            store(chain, product(moves[high], step))

    store(moves.at[high], product(high_ref[...], moves[low]))
    for place in range(2):
        store(factors.at[place], product(moves[place], self_ref[...]))


def far_matrices(slab, chain, far_self, far_partner, coupling, high, goes_on):
    n = coupling.shape[0]
    matrix = jax.ShapeDtypeStruct((2 * n, n), BF16)
    pair = jax.ShapeDtypeStruct((2, 2 * n, n), BF16)
    return call(
        far_matrices_kernel,
        [pair, pair] + [matrix] * goes_on,
        [SMEM] + [VMEM] * 5,
        vmem=24,
        cost=5.2,
    )(slab, chain, far_self, far_partner, coupling, high)


def block_start(place, group, n, energies):
    first, last = group
    size = n * (last - first) // energies
    return size, pl.multiple_of((place ^ first) // (last - first) * size, size)


def moved_rows(rows, move):
    n = move.shape[0] // 2
    return complex_of(mxu_nt(rows, move[:n]), mxu_nt(rows, move[n:]))


def moved_term(rows, move, factor):
    moved = [part.astype(BF16) for part in moved_rows(rows, move)]
    return complex_of(mxu(factor, moved[0]), mxu(factor, moved[1]))


def own_terms_kernel(place_ref, high_ref, own_ref, factor_ref, *refs, groups, energies):
    chunks, (self_ref, partner_ref, rows_ref) = refs[:-3], refs[-3:]
    n = self_ref.shape[1]
    for group, chunk in zip(groups, chunks):
        size, start = block_start(place_ref[0], group, n, energies)
        for part in range(2):
            at = pl.ds(pl.multiple_of(part * n + start, size), size)
            rows_ref[at, :] = chunk[part * size : (part + 1) * size, :]
    store(partner_ref, moved_term(rows_ref[...], high_ref[...], factor_ref[...]))
    store(self_ref, product(own_ref[...], rows_ref[...]))


def own_terms(place, high, own, factor, chunks, groups, energies):
    n = own.shape[1]
    total = jax.ShapeDtypeStruct((2 * n, n), F32)
    return call(
        functools.partial(own_terms_kernel, groups=groups, energies=energies),
        [total, total],
        [SMEM] + [VMEM] * (3 + len(chunks)),
        [pltpu.VMEM((2 * n, n), BF16)],
        vmem=20,
        cost=3.6,
    )(place, high, own, factor, *chunks)


def far_terms_kernel(place_ref, total_ref, *refs, target, group, energies):
    out_ref, refs = refs[-1], refs[:-1]
    n = total_ref.shape[1]
    total = [total_ref[:n, :], total_ref[n:, :]]
    size, start = block_start(place_ref[0], group, n, energies)
    for term in range(len(refs) // 3):
        block, moves, factors = refs[3 * term : 3 * term + 3]
        factor = factors.at[target]
        parts = moved_term(block[: 2 * size, :], moves[target], factor[:, pl.ds(start, size)])
        total = [a + b for a, b in zip(total, parts)]
    store(out_ref, total)


def far_terms(place, total, terms, group, target, dtype, energies):
    n = total.shape[1]
    arrays = [array for term in terms for array in term]
    return call(
        functools.partial(far_terms_kernel, target=target, group=group, energies=energies),
        jax.ShapeDtypeStruct((2 * n, n), dtype),
        [SMEM] + [VMEM] * (1 + len(arrays)),
        vmem=20 + 5 * (len(terms) - 1),
        cost=1.8,
    )(place, total, *arrays)


def diagonal_kernel(place_ref, inverse_ref, high_ref, factor_ref, rows_ref, *refs, rows):
    out_ref, refs = refs[-1], refs[:-1]
    n = rows_ref.shape[1]
    pick = (
        lax.broadcasted_iota(jnp.int32, (rows, n), 0) + place_ref[0] * rows
        == lax.broadcasted_iota(jnp.int32, (rows, n), 1)
    ).astype(BF16)

    def part(first, second):
        real, imag = mxu_nt(pick, first[:n]), mxu_nt(pick, first[n:])
        return jnp.sum(real * second[1] + imag * second[0], axis=0, keepdims=True)

    block = rows_ref[...]
    sums = [
        part(inverse_ref[...], (block[:rows].astype(F32), block[rows:].astype(F32))),
        part(factor_ref[...], moved_rows(block, high_ref[...])),
    ]
    for far in range(len(refs) // 3):
        far_ref, moves, factors = refs[3 * far : 3 * far + 3]
        block = far_ref[...]
        for target in range(2):
            sums[target] += part(factors[target], moved_rows(block, moves[target]))
    for target in range(2):
        out_ref[target : target + 1, :] = sums[target]


def diagonal_sums(place, inverse, high, factor, rows, far, energies):
    n = inverse.shape[1]
    arrays = [array for term in far for array in term]
    return call(
        functools.partial(diagonal_kernel, rows=n // energies),
        jax.ShapeDtypeStruct((2, n), F32),
        [SMEM] + [VMEM] * (4 + len(arrays)),
        vmem=20 + 5 * (len(far) - 1),
        cost=2.4,
    )(place, inverse, high, factor, rows, *arrays)


def add_kernel(first_ref, second_ref, out_ref):
    out_ref[...] = first_ref[...] + second_ref[...]


def add(first, second):
    shape = jax.ShapeDtypeStruct(first.shape, first.dtype)
    return call(add_kernel, shape, [VMEM] * 2, vmem=4)(first, second)


def finish_kernel(own_ref, partner_ref, own_density_ref, partner_density_ref, green_ref, density_ref):
    green_ref[...] = (own_ref[...] + partner_ref[...].astype(F32)).astype(BF16)
    density_ref[...] = -(own_density_ref[0:1, :] + partner_density_ref[1:2, :])


def finish(own, partner, own_density, partner_density):
    n = own.shape[1]
    return call(
        finish_kernel,
        [jax.ShapeDtypeStruct((2 * n, n), BF16), jax.ShapeDtypeStruct((1, n), F32)],
        [VMEM] * 4,
        cost=1.2,
    )(own, partner, own_density, partner_density)


def exchange(x, axis, distance):
    size = lax.axis_size(axis)
    return lax.ppermute(x, axis, [(i, i ^ distance) for i in range(size)])


def shift(x, axis, by):
    size = lax.axis_size(axis)
    return lax.ppermute(x, axis, [(i, i + by) for i in range(size - by)])


def after(x, *others):
    return lax.optimization_barrier((x, *others))[0]


def exchange_all(pieces, order, window):
    received = list(pieces)
    for at, distance in enumerate(order):
        piece = pieces[distance]
        if at >= window:
            piece = after(piece, received[order[at - window]])
        received[distance] = exchange(piece, "energy", distance)
    return received


def local(
    green_prev,
    slab_inverse,
    coupling_block,
    phonon_coupling,
    offset,
    occupation,
    pair_source,
    pair_mode,
    active_slabs,
):
    energies = pair_source.shape[0]
    n = coupling_block.shape[0]
    rows = n // energies
    slabs = lax.axis_size("slab")
    place = lax.axis_index("energy").astype(jnp.int32)
    slab = lax.axis_index("slab").astype(jnp.int32)
    core = slab & 1
    place_one = place[None]
    slab_one = slab[None]
    column = slab_inverse[0].reshape(2 * n, n)
    green = green_prev[0, 0]

    half = energies // 2
    partner = exchange(column, "slab", 1)
    far_selves = [shift(column, "slab", behind) for behind in range(2, slabs, 2)]
    weights = weight_rows(slab_one, active_slabs, occupation, offset, n)
    sent = [
        jnp.concatenate(
            [lax.dynamic_slice_in_dim(part, (place ^ distance) * rows, rows) for part in green]
            + [weights]
        )
        for distance in range(energies)
    ]
    sent[1] = after(sent[1], partner)
    pieces = exchange_all(sent, range(1, energies), energies)
    low_move, high_move, own_factor = own_matrices(slab_one, column, partner, coupling_block)
    pieces[0] = after(pieces[0], high_move)
    *mixed, weighted, totals = mix(place_one, pair_source, pair_mode, phonon_coupling, pieces)
    far_partners = [exchange(after(far_self, mixed[1]), "slab", 1) for far_self in far_selves]
    back = exchange_all(mixed, range(1, energies), energies)
    back[1] = after(back[1], *far_partners)

    scalars = (place_one, slab_one, active_slabs, offset)
    near, cross = (0, half), (half, energies)
    own_weighted = weighted_rows(place_one, column, weighted, totals)
    far_weighted = [shift(own_weighted, "slab", behind) for behind in range(2, slabs, 2)]
    back[0] = after(back[0], own_weighted)
    own_near = right_rows(scalars, column, back[:half], 0)

    chain = after(low_move, own_near, *far_weighted)
    far = []
    for index, (far_self, far_partner) in enumerate(zip(far_selves, far_partners)):
        moves, factors, *chain = far_matrices(
            slab_one,
            chain if index == 0 else chain[0],
            far_self,
            far_partner,
            coupling_block,
            high_move,
            index + 1 < len(far_selves),
        )
        far.append((moves, factors))
    density = diagonal_sums(
        place_one,
        column,
        high_move,
        own_factor,
        own_weighted,
        [(rows, *matrices) for rows, matrices in zip(far_weighted, far)],
        energies,
    )

    back[half] = after(back[half], density)
    own_cross = right_rows(scalars, column, back[half:], half)
    far_near = [shift(own_near, "slab", behind) for behind in range(2, slabs, 2)]
    far_cross = [shift(own_cross, "slab", behind) for behind in range(2, slabs, 2)]

    for_self, for_partner = own_terms(
        place_one, high_move, column, own_factor, [own_near, own_cross], (near, cross), energies
    )
    near_terms = [(rows, *matrices) for rows, matrices in zip(far_near, far)]
    cross_terms = [(rows, *matrices) for rows, matrices in zip(far_cross, far)]
    def energy_step(density, distance):
        return add(density, exchange(density, "energy", distance))

    def far_sum(total, terms, group, target, dtype=F32):
        return far_terms(place_one, total, terms, group, target, dtype, energies) if terms else total

    distances = [1 << bit for bit in range(energies.bit_length() - 1)]
    density = energy_step(density, distances[0])
    for_partner = far_sum(for_partner, near_terms, near, 1)
    for_self = far_sum(after(for_self, density), near_terms, near, 0)
    density = energy_step(density, distances[1])
    for_partner = far_sum(after(for_partner, density, for_self), cross_terms, cross, 1, BF16).astype(BF16)
    for distance in distances[2:]:
        density = energy_step(density, distance)
    from_partner = exchange(for_partner, "slab", 1)
    density_partner = exchange(density, "slab", 1)
    for_self = far_sum(for_self, cross_terms, cross, 0)
    current, density = finish(for_self, from_partner, density, density_partner)
    return (current.reshape(1, 1, 2, n, n), density)


def solution(mesh):
    in_specs = (
        P("energy", "slab", None, None, None),
        P("slab", None, None, None),
        P(),
        P(None, "energy", None),
        P("energy"),
        P("energy"),
        P(),
        P(),
        P("energy"),
    )
    out_specs = (P("energy", "slab", None, None, None), P("slab", None))
    return jax.shard_map(local, mesh=mesh, in_specs=in_specs, out_specs=out_specs, check_vma=False)
```

```python
import functools

import jax
import jax.numpy as jnp
from jax import lax
from jax.experimental import pallas as pl
from jax.experimental.pallas import tpu as pltpu
from jax.sharding import PartitionSpec as P

BF16 = jnp.bfloat16
F32 = jnp.float32
LANES = 128
MICROSECOND = 3_300_000
VMEM = pl.BlockSpec(memory_space=pltpu.VMEM)
SMEM = pl.BlockSpec(memory_space=pltpu.SMEM)


def mxu(first, second):
    return jnp.dot(first, second, preferred_element_type=F32)


def mxu_nt(first, second):
    return lax.dot_general(first, second, (((1,), (1,)), ((), ())), preferred_element_type=F32)


def call(kernel, out_shape, in_specs, scratch=(), vmem=16, cost=0.0):
    return pl.pallas_call(
        kernel,
        out_shape=out_shape,
        in_specs=in_specs,
        out_specs=jax.tree.map(lambda _: VMEM, out_shape),
        scratch_shapes=list(scratch),
        compiler_params=pltpu.CompilerParams(vmem_limit_bytes=vmem * 2**20),
        cost_estimate=pl.CostEstimate(
            flops=1024, bytes_accessed=1024 + int(cost * MICROSECOND), transcendentals=0
        ),
    )


def complex_of(by_real, by_imag):
    rows = by_real.shape[0] // 2
    return by_real[:rows] - by_imag[rows:], by_real[rows:] + by_imag[:rows]


def product(first, second):
    rows = second.shape[0] // 2
    return complex_of(mxu(first, second[:rows]), mxu(first, second[rows:]))


def store(ref, parts):
    rows = parts[0].shape[0]
    for index, part in enumerate(parts):
        ref[index * rows : (index + 1) * rows, :] = part.astype(ref.dtype)


def weight_kernel(slab_ref, active_ref, occupation_ref, offset_ref, out_ref):
    shape = out_ref.shape
    row = lax.broadcasted_iota(jnp.int32, shape, 0)
    lane = lax.broadcasted_iota(jnp.int32, shape, 1)
    weight = occupation_ref[0]
    active = jnp.where(slab_ref[0] < active_ref[0], weight, 0.0)
    rest = jnp.where(lane < 2 * LANES, weight, weight * offset_ref[0])
    rest = jnp.where(lane < LANES, active, rest)
    out = jnp.zeros(shape, F32)
    for index in range(3):
        part = rest.astype(BF16).astype(F32)
        out = jnp.where(row == index, part, out)
        rest = rest - part
    out_ref[...] = out.astype(BF16)


def weight_rows(slab, active, occupation, offset, n):
    shape = jax.ShapeDtypeStruct((8, n), BF16)
    return call(weight_kernel, shape, [SMEM] * 4, vmem=4)(slab, active, occupation, offset)


def wide(row, n):
    return jnp.concatenate([row[:, :LANES]] * (n // LANES), axis=1)


def mix_kernel(place_ref, source_ref, mode_ref, phonon_ref, *refs):
    energies = (len(refs) - 5) // 2
    pieces, outs = refs[:energies], refs[energies : 2 * energies]
    weighted_ref, totals_ref, green, phonon, weights = refs[2 * energies :]
    place = place_ref[0]
    pairs = source_ref.shape[1]
    rows, n = phonon_ref.shape[1:]
    phonon[...] = phonon_ref[...].astype(F32)
    totals = jnp.zeros((1, n), F32)
    for distance in range(energies):
        piece = pieces[distance]
        for part in range(2):
            green[place ^ distance, part] = piece[part * rows : (part + 1) * rows, :].astype(F32)
        parts = piece[2 * rows :, :].astype(F32)
        row = parts[0:1] + parts[1:2] + parts[2:3]
        totals = totals + row
        weights[place ^ distance] = jnp.broadcast_to(wide(row, n), (8, n))
    totals_ref[...] = jnp.broadcast_to(totals, totals_ref.shape)
    step = 16

    @pl.loop(0, rows // step)
    def _(block):
        at = pl.ds(pl.multiple_of(block * step, step), step)
        weighted_real = jnp.zeros((step, n), F32)
        weighted_imag = jnp.zeros((step, n), F32)
        for distance in range(energies):
            energy = place ^ distance
            real = jnp.zeros((step, n), F32)
            imag = jnp.zeros((step, n), F32)
            for pair in range(pairs):
                origin = source_ref[energy, pair]
                factor = phonon[mode_ref[energy, pair], at, :]
                real = real + factor * green[origin, 0, at, :]
                imag = imag + factor * green[origin, 1, at, :]
            outs[distance][0, at, :] = real.astype(BF16)
            outs[distance][1, at, :] = imag.astype(BF16)
            weight = weights[energy, 0:1, :]
            weighted_real = weighted_real + weight * real
            weighted_imag = weighted_imag + weight * imag
        weighted_ref[0, at, :] = weighted_real.astype(BF16)
        weighted_ref[1, at, :] = weighted_imag.astype(BF16)


def mix(place, source, mode, phonon, pieces):
    energies = len(pieces)
    _, rows, n = phonon.shape
    block = jax.ShapeDtypeStruct((2, rows, n), BF16)
    return call(
        mix_kernel,
        [block] * (energies + 1) + [jax.ShapeDtypeStruct((8, n), F32)],
        [SMEM] * 3 + [VMEM] * (energies + 1),
        [
            pltpu.VMEM((energies, 2, rows, n), F32),
            pltpu.VMEM(phonon.shape, F32),
            pltpu.VMEM((energies, 8, n), F32),
        ],
        vmem=12,
        cost=2.0,
    )(place, source, mode, phonon, *pieces)


def finished_rows(sigma, inverse_ref, start, mask, offset, one):
    size, n = sigma.shape[0] // 2, sigma.shape[1]
    eye = (
        lax.broadcasted_iota(jnp.int32, (size, n), 0) + start
        == lax.broadcasted_iota(jnp.int32, (size, n), 1)
    ).astype(F32)
    real, imag = product(sigma, inverse_ref[...])
    own_real = inverse_ref[pl.ds(start, size), :].astype(F32)
    own_imag = inverse_ref[pl.ds(pl.multiple_of(n + start, size), size), :].astype(F32)
    return mask * real + offset * own_real + one * eye, mask * imag + offset * own_imag


def right_kernel(place_ref, slab_ref, active_ref, offset_ref, inverse_ref, *refs, first):
    pieces, out_ref, rows_ref = refs[:-2], refs[-2], refs[-1]
    count = len(pieces)
    place = place_ref[0] ^ first
    rows = pieces[0].shape[1]
    total = count * rows
    for index, piece in enumerate(pieces):
        at = (place ^ index) & (count - 1)
        for part in range(2):
            rows_ref[pl.ds(pl.multiple_of(part * total + at * rows, rows), rows), :] = piece[part]
    mask = jnp.where(slab_ref[0] < active_ref[0], 1.0, 0.0)
    start = pl.multiple_of(place // count * total, total)
    store(out_ref, finished_rows(rows_ref[...], inverse_ref, start, mask, offset_ref[0], 1.0))


def right_rows(scalars, inverse, pieces, first):
    _, rows, n = pieces[0].shape
    total = rows * len(pieces)
    return call(
        functools.partial(right_kernel, first=first),
        jax.ShapeDtypeStruct((2 * total, n), BF16),
        [SMEM] * 4 + [VMEM] * (1 + len(pieces)),
        [pltpu.VMEM((2 * total, n), BF16)],
        vmem=12,
        cost=0.8,
    )(*scalars, inverse, *pieces)


def weighted_kernel(place_ref, inverse_ref, sigma_ref, totals_ref, out_ref):
    _, rows, n = sigma_ref.shape
    start = pl.multiple_of(place_ref[0] * rows, rows)
    one = wide(totals_ref[0:1, LANES : 2 * LANES], n)
    offset = wide(totals_ref[0:1, 2 * LANES : 3 * LANES], n)
    sigma = sigma_ref[...].reshape(2 * rows, n)
    store(out_ref, finished_rows(sigma, inverse_ref, start, 1.0, offset, one))


def weighted_rows(place, inverse, sigma, totals):
    _, rows, n = sigma.shape
    return call(
        weighted_kernel,
        jax.ShapeDtypeStruct((2 * rows, n), BF16),
        [SMEM] + [VMEM] * 3,
        vmem=8,
        cost=0.3,
    )(place, inverse, sigma, totals)


def own_matrices_kernel(slab_ref, self_ref, partner_ref, coupling_ref, low_ref, high_ref, factor_ref, both):
    core = slab_ref[0] & 1
    both[core] = self_ref[...]
    both[1 - core] = partner_ref[...]
    coupling = coupling_ref[...]
    low_ref[...] = mxu(both[0], coupling).astype(BF16)
    high_ref[...] = mxu(both[1], coupling).astype(BF16)

    @pl.when(core == 0)
    def _():
        store(factor_ref, product(high_ref[...], self_ref[...]))

    @pl.when(core != 0)
    def _():
        factor_ref[...] = jnp.zeros_like(factor_ref)


def own_matrices(slab, own, partner, coupling):
    n = coupling.shape[0]
    matrix = jax.ShapeDtypeStruct((2 * n, n), BF16)
    return call(
        own_matrices_kernel,
        [matrix, matrix, matrix],
        [SMEM] + [VMEM] * 3,
        [pltpu.VMEM((2, 2 * n, n), BF16)],
        vmem=20,
        cost=0.0,
    )(slab, own, partner, coupling)


def far_matrices_kernel(slab_ref, chain_ref, self_ref, partner_ref, coupling_ref, high_ref, moves, factors, *more):
    core = slab_ref[0] & 1
    low, high = core, 1 - core

    def chain_and_high(high_inverse):
        step = mxu(high_inverse, coupling_ref[...]).astype(BF16)
        store(moves.at[high], product(chain_ref[...], step))

    @pl.when(core == 0)
    def _():
        chain_and_high(partner_ref[...])
        moves[low] = moves[high]
        for chain in more:
            step = mxu(self_ref[...], coupling_ref[...]).astype(BF16)
            store(chain, product(moves[high], step))

    @pl.when(core != 0)
    def _():
        moves[low] = chain_ref[...]
        for chain in more:
            chain_and_high(self_ref[...])
            step = mxu(partner_ref[...], coupling_ref[...]).astype(BF16)
            store(chain, product(moves[high], step))

    store(moves.at[high], product(high_ref[...], moves[low]))
    for place in range(2):
        store(factors.at[place], product(moves[place], self_ref[...]))


def far_matrices(slab, chain, far_self, far_partner, coupling, high, goes_on):
    n = coupling.shape[0]
    matrix = jax.ShapeDtypeStruct((2 * n, n), BF16)
    pair = jax.ShapeDtypeStruct((2, 2 * n, n), BF16)
    return call(
        far_matrices_kernel,
        [pair, pair] + [matrix] * goes_on,
        [SMEM] + [VMEM] * 5,
        vmem=24,
        cost=5.2,
    )(slab, chain, far_self, far_partner, coupling, high)


def block_start(place, group, n, energies):
    first, last = group
    size = n * (last - first) // energies
    return size, pl.multiple_of((place ^ first) // (last - first) * size, size)


def moved_rows(rows, move):
    n = move.shape[0] // 2
    return complex_of(mxu_nt(rows, move[:n]), mxu_nt(rows, move[n:]))


def moved_term(rows, move, factor):
    moved = [part.astype(BF16) for part in moved_rows(rows, move)]
    return complex_of(mxu(factor, moved[0]), mxu(factor, moved[1]))


def own_terms_kernel(place_ref, high_ref, own_ref, factor_ref, *refs, groups, energies):
    chunks, (self_ref, partner_ref, rows_ref) = refs[:-3], refs[-3:]
    n = self_ref.shape[1]
    for group, chunk in zip(groups, chunks):
        size, start = block_start(place_ref[0], group, n, energies)
        for part in range(2):
            at = pl.ds(pl.multiple_of(part * n + start, size), size)
            rows_ref[at, :] = chunk[part * size : (part + 1) * size, :]
    store(partner_ref, moved_term(rows_ref[...], high_ref[...], factor_ref[...]))
    store(self_ref, product(own_ref[...], rows_ref[...]))


def own_terms(place, high, own, factor, chunks, groups, energies):
    n = own.shape[1]
    total = jax.ShapeDtypeStruct((2 * n, n), F32)
    return call(
        functools.partial(own_terms_kernel, groups=groups, energies=energies),
        [total, total],
        [SMEM] + [VMEM] * (3 + len(chunks)),
        [pltpu.VMEM((2 * n, n), BF16)],
        vmem=20,
        cost=3.6,
    )(place, high, own, factor, *chunks)


def far_terms_kernel(place_ref, total_ref, *refs, target, group, energies):
    out_ref, refs = refs[-1], refs[:-1]
    n = total_ref.shape[1]
    total = [total_ref[:n, :], total_ref[n:, :]]
    size, start = block_start(place_ref[0], group, n, energies)
    for term in range(len(refs) // 3):
        block, moves, factors = refs[3 * term : 3 * term + 3]
        factor = factors.at[target]
        parts = moved_term(block[: 2 * size, :], moves[target], factor[:, pl.ds(start, size)])
        total = [a + b for a, b in zip(total, parts)]
    store(out_ref, total)


def far_terms(place, total, terms, group, target, dtype, energies):
    n = total.shape[1]
    arrays = [array for term in terms for array in term]
    return call(
        functools.partial(far_terms_kernel, target=target, group=group, energies=energies),
        jax.ShapeDtypeStruct((2 * n, n), dtype),
        [SMEM] + [VMEM] * (1 + len(arrays)),
        vmem=20 + 5 * (len(terms) - 1),
        cost=1.8,
    )(place, total, *arrays)


def diagonal_kernel(place_ref, inverse_ref, high_ref, factor_ref, rows_ref, *refs, rows):
    out_ref, refs = refs[-1], refs[:-1]
    n = rows_ref.shape[1]
    pick = (
        lax.broadcasted_iota(jnp.int32, (rows, n), 0) + place_ref[0] * rows
        == lax.broadcasted_iota(jnp.int32, (rows, n), 1)
    ).astype(BF16)

    def part(first, second):
        real, imag = mxu_nt(pick, first[:n]), mxu_nt(pick, first[n:])
        return jnp.sum(real * second[1] + imag * second[0], axis=0, keepdims=True)

    block = rows_ref[...]
    sums = [
        part(inverse_ref[...], (block[:rows].astype(F32), block[rows:].astype(F32))),
        part(factor_ref[...], moved_rows(block, high_ref[...])),
    ]
    for far in range(len(refs) // 3):
        far_ref, moves, factors = refs[3 * far : 3 * far + 3]
        block = far_ref[...]
        for target in range(2):
            sums[target] += part(factors[target], moved_rows(block, moves[target]))
    for target in range(2):
        out_ref[target : target + 1, :] = sums[target]


def diagonal_sums(place, inverse, high, factor, rows, far, energies):
    n = inverse.shape[1]
    arrays = [array for term in far for array in term]
    return call(
        functools.partial(diagonal_kernel, rows=n // energies),
        jax.ShapeDtypeStruct((2, n), F32),
        [SMEM] + [VMEM] * (4 + len(arrays)),
        vmem=20 + 5 * (len(far) - 1),
        cost=2.4,
    )(place, inverse, high, factor, rows, *arrays)


def add_kernel(first_ref, second_ref, out_ref):
    out_ref[...] = first_ref[...] + second_ref[...]


def add(first, second):
    shape = jax.ShapeDtypeStruct(first.shape, first.dtype)
    return call(add_kernel, shape, [VMEM] * 2, vmem=4)(first, second)


def finish_kernel(own_ref, partner_ref, own_density_ref, partner_density_ref, green_ref, density_ref):
    green_ref[...] = (own_ref[...] + partner_ref[...].astype(F32)).astype(BF16)
    density_ref[...] = -(own_density_ref[0:1, :] + partner_density_ref[1:2, :])


def finish(own, partner, own_density, partner_density):
    n = own.shape[1]
    return call(
        finish_kernel,
        [jax.ShapeDtypeStruct((2 * n, n), BF16), jax.ShapeDtypeStruct((1, n), F32)],
        [VMEM] * 4,
        cost=1.2,
    )(own, partner, own_density, partner_density)


def exchange(x, axis, distance):
    size = lax.axis_size(axis)
    return lax.ppermute(x, axis, [(i, i ^ distance) for i in range(size)])


def shift(x, axis, by):
    size = lax.axis_size(axis)
    return lax.ppermute(x, axis, [(i, i + by) for i in range(size - by)])


def after(x, *others):
    return lax.optimization_barrier((x, *others))[0]


def exchange_all(pieces, order, window):
    received = list(pieces)
    for at, distance in enumerate(order):
        piece = pieces[distance]
        if at >= window:
            piece = after(piece, received[order[at - window]])
        received[distance] = exchange(piece, "energy", distance)
    return received


def local(
    green_prev,
    slab_inverse,
    coupling_block,
    phonon_coupling,
    offset,
    occupation,
    pair_source,
    pair_mode,
    active_slabs,
):
    energies = pair_source.shape[0]
    n = coupling_block.shape[0]
    rows = n // energies
    slabs = lax.axis_size("slab")
    place = lax.axis_index("energy").astype(jnp.int32)
    slab = lax.axis_index("slab").astype(jnp.int32)
    core = slab & 1
    place_one = place[None]
    slab_one = slab[None]
    column = slab_inverse[0].reshape(2 * n, n)
    green = green_prev[0, 0]

    half = energies // 2
    partner = exchange(column, "slab", 1)
    far_selves = [shift(column, "slab", behind) for behind in range(2, slabs, 2)]
    weights = weight_rows(slab_one, active_slabs, occupation, offset, n)
    sent = [
        jnp.concatenate(
            [lax.dynamic_slice_in_dim(part, (place ^ distance) * rows, rows) for part in green]
            + [weights]
        )
        for distance in range(energies)
    ]
    sent[1] = after(sent[1], partner)
    pieces = exchange_all(sent, range(1, energies), energies)
    low_move, high_move, own_factor = own_matrices(slab_one, column, partner, coupling_block)
    pieces[0] = after(pieces[0], high_move)
    *mixed, weighted, totals = mix(place_one, pair_source, pair_mode, phonon_coupling, pieces)
    far_partners = [exchange(after(far_self, mixed[1]), "slab", 1) for far_self in far_selves]
    back = exchange_all(mixed, range(1, energies), energies)
    back[1] = after(back[1], *far_partners)

    scalars = (place_one, slab_one, active_slabs, offset)
    near, cross = (0, half), (half, energies)
    own_weighted = weighted_rows(place_one, column, weighted, totals)
    far_weighted = [shift(own_weighted, "slab", behind) for behind in range(2, slabs, 2)]
    back[0] = after(back[0], own_weighted)
    own_near = right_rows(scalars, column, back[:half], 0)

    chain = after(low_move, own_near, *far_weighted)
    far = []
    for index, (far_self, far_partner) in enumerate(zip(far_selves, far_partners)):
        moves, factors, *chain = far_matrices(
            slab_one,
            chain if index == 0 else chain[0],
            far_self,
            far_partner,
            coupling_block,
            high_move,
            index + 1 < len(far_selves),
        )
        far.append((moves, factors))
    density = diagonal_sums(
        place_one,
        column,
        high_move,
        own_factor,
        own_weighted,
        [(rows, *matrices) for rows, matrices in zip(far_weighted, far)],
        energies,
    )

    def energy_step(density, distance):
        return add(density, exchange(density, "energy", distance))

    distances = [1 << bit for bit in range(energies.bit_length() - 1)]
    early = 1
    density = after(density, back[half])
    for distance in distances[:early]:
        density = energy_step(density, distance)
    back[half] = after(back[half], density)
    own_cross = right_rows(scalars, column, back[half:], half)
    far_near = [shift(own_near, "slab", behind) for behind in range(2, slabs, 2)]
    far_cross = [shift(own_cross, "slab", behind) for behind in range(2, slabs, 2)]

    for_self, for_partner = own_terms(
        place_one, high_move, column, own_factor, [own_near, own_cross], (near, cross), energies
    )
    near_terms = [(rows, *matrices) for rows, matrices in zip(far_near, far)]
    cross_terms = [(rows, *matrices) for rows, matrices in zip(far_cross, far)]
    def far_sum(total, terms, group, target, dtype=F32):
        return far_terms(place_one, total, terms, group, target, dtype, energies) if terms else total

    for_partner = far_sum(for_partner, near_terms, near, 1)
    for_self = far_sum(for_self, near_terms, near, 0)
    for distance in distances[early:]:
        density = energy_step(density, distance)
    for_partner = far_sum(after(for_partner, density, for_self), cross_terms, cross, 1, BF16).astype(BF16)
    from_partner = exchange(for_partner, "slab", 1)
    density_partner = exchange(density, "slab", 1)
    for_self = far_sum(for_self, cross_terms, cross, 0)
    current, density = finish(for_self, from_partner, density, density_partner)
    return (current.reshape(1, 1, 2, n, n), density)


def solution(mesh):
    in_specs = (
        P("energy", "slab", None, None, None),
        P("slab", None, None, None),
        P(),
        P(None, "energy", None),
        P("energy"),
        P("energy"),
        P(),
        P(),
        P("energy"),
    )
    out_specs = (P("energy", "slab", None, None, None), P("slab", None))
    return jax.shard_map(local, mesh=mesh, in_specs=in_specs, out_specs=out_specs, check_vma=False)
```

```python
import functools

import jax
import jax.numpy as jnp
from jax import lax
from jax.experimental import pallas as pl
from jax.experimental.pallas import tpu as pltpu
from jax.sharding import PartitionSpec as P

BF16 = jnp.bfloat16
F32 = jnp.float32
LANES = 128
MICROSECOND = 3_300_000
VMEM = pl.BlockSpec(memory_space=pltpu.VMEM)
SMEM = pl.BlockSpec(memory_space=pltpu.SMEM)


def mxu(first, second):
    return jnp.dot(first, second, preferred_element_type=F32)


def mxu_nt(first, second):
    return lax.dot_general(first, second, (((1,), (1,)), ((), ())), preferred_element_type=F32)


def call(kernel, out_shape, in_specs, scratch=(), vmem=16, cost=0.0):
    return pl.pallas_call(
        kernel,
        out_shape=out_shape,
        in_specs=in_specs,
        out_specs=jax.tree.map(lambda _: VMEM, out_shape),
        scratch_shapes=list(scratch),
        compiler_params=pltpu.CompilerParams(vmem_limit_bytes=vmem * 2**20),
        cost_estimate=pl.CostEstimate(
            flops=1024, bytes_accessed=1024 + int(cost * MICROSECOND), transcendentals=0
        ),
    )


def complex_of(by_real, by_imag):
    rows = by_real.shape[0] // 2
    return by_real[:rows] - by_imag[rows:], by_real[rows:] + by_imag[:rows]


def product(first, second):
    rows = second.shape[0] // 2
    return complex_of(mxu(first, second[:rows]), mxu(first, second[rows:]))


def store(ref, parts):
    rows = parts[0].shape[0]
    for index, part in enumerate(parts):
        ref[index * rows : (index + 1) * rows, :] = part.astype(ref.dtype)


def weight_kernel(slab_ref, active_ref, occupation_ref, offset_ref, out_ref):
    shape = out_ref.shape
    row = lax.broadcasted_iota(jnp.int32, shape, 0)
    lane = lax.broadcasted_iota(jnp.int32, shape, 1)
    weight = occupation_ref[0]
    active = jnp.where(slab_ref[0] < active_ref[0], weight, 0.0)
    rest = jnp.where(lane < 2 * LANES, weight, weight * offset_ref[0])
    rest = jnp.where(lane < LANES, active, rest)
    out = jnp.zeros(shape, F32)
    for index in range(3):
        part = rest.astype(BF16).astype(F32)
        out = jnp.where(row == index, part, out)
        rest = rest - part
    out_ref[...] = out.astype(BF16)


def weight_rows(slab, active, occupation, offset, n):
    shape = jax.ShapeDtypeStruct((8, n), BF16)
    return call(weight_kernel, shape, [SMEM] * 4, vmem=4)(slab, active, occupation, offset)


def wide(row, n):
    return jnp.concatenate([row[:, :LANES]] * (n // LANES), axis=1)


def mix_kernel(place_ref, source_ref, mode_ref, phonon_ref, *refs):
    energies = (len(refs) - 5) // 2
    pieces, outs = refs[:energies], refs[energies : 2 * energies]
    weighted_ref, totals_ref, green, phonon, weights = refs[2 * energies :]
    place = place_ref[0]
    pairs = source_ref.shape[1]
    rows, n = phonon_ref.shape[1:]
    phonon[...] = phonon_ref[...].astype(F32)
    totals = jnp.zeros((1, n), F32)
    for distance in range(energies):
        piece = pieces[distance]
        for part in range(2):
            green[place ^ distance, part] = piece[part * rows : (part + 1) * rows, :].astype(F32)
        parts = piece[2 * rows :, :].astype(F32)
        row = parts[0:1] + parts[1:2] + parts[2:3]
        totals = totals + row
        weights[place ^ distance] = jnp.broadcast_to(wide(row, n), (8, n))
    totals_ref[...] = jnp.broadcast_to(totals, totals_ref.shape)
    step = 16

    @pl.loop(0, rows // step)
    def _(block):
        at = pl.ds(pl.multiple_of(block * step, step), step)
        weighted_real = jnp.zeros((step, n), F32)
        weighted_imag = jnp.zeros((step, n), F32)
        for distance in range(energies):
            energy = place ^ distance
            real = jnp.zeros((step, n), F32)
            imag = jnp.zeros((step, n), F32)
            for pair in range(pairs):
                origin = source_ref[energy, pair]
                factor = phonon[mode_ref[energy, pair], at, :]
                real = real + factor * green[origin, 0, at, :]
                imag = imag + factor * green[origin, 1, at, :]
            outs[distance][0, at, :] = real.astype(BF16)
            outs[distance][1, at, :] = imag.astype(BF16)
            weight = weights[energy, 0:1, :]
            weighted_real = weighted_real + weight * real
            weighted_imag = weighted_imag + weight * imag
        weighted_ref[0, at, :] = weighted_real.astype(BF16)
        weighted_ref[1, at, :] = weighted_imag.astype(BF16)


def mix(place, source, mode, phonon, pieces):
    energies = len(pieces)
    _, rows, n = phonon.shape
    block = jax.ShapeDtypeStruct((2, rows, n), BF16)
    return call(
        mix_kernel,
        [block] * (energies + 1) + [jax.ShapeDtypeStruct((8, n), F32)],
        [SMEM] * 3 + [VMEM] * (energies + 1),
        [
            pltpu.VMEM((energies, 2, rows, n), F32),
            pltpu.VMEM(phonon.shape, F32),
            pltpu.VMEM((energies, 8, n), F32),
        ],
        vmem=12,
        cost=2.0,
    )(place, source, mode, phonon, *pieces)


def finished_rows(sigma, inverse_ref, start, mask, offset, one):
    size, n = sigma.shape[0] // 2, sigma.shape[1]
    eye = (
        lax.broadcasted_iota(jnp.int32, (size, n), 0) + start
        == lax.broadcasted_iota(jnp.int32, (size, n), 1)
    ).astype(F32)
    real, imag = product(sigma, inverse_ref[...])
    own_real = inverse_ref[pl.ds(start, size), :].astype(F32)
    own_imag = inverse_ref[pl.ds(pl.multiple_of(n + start, size), size), :].astype(F32)
    return mask * real + offset * own_real + one * eye, mask * imag + offset * own_imag


def right_kernel(place_ref, slab_ref, active_ref, offset_ref, inverse_ref, *refs, first):
    pieces, out_ref, rows_ref = refs[:-2], refs[-2], refs[-1]
    count = len(pieces)
    place = place_ref[0] ^ first
    rows = pieces[0].shape[1]
    total = count * rows
    for index, piece in enumerate(pieces):
        at = (place ^ index) & (count - 1)
        for part in range(2):
            rows_ref[pl.ds(pl.multiple_of(part * total + at * rows, rows), rows), :] = piece[part]
    mask = jnp.where(slab_ref[0] < active_ref[0], 1.0, 0.0)
    start = pl.multiple_of(place // count * total, total)
    store(out_ref, finished_rows(rows_ref[...], inverse_ref, start, mask, offset_ref[0], 1.0))


def right_rows(scalars, inverse, pieces, first):
    _, rows, n = pieces[0].shape
    total = rows * len(pieces)
    return call(
        functools.partial(right_kernel, first=first),
        jax.ShapeDtypeStruct((2 * total, n), BF16),
        [SMEM] * 4 + [VMEM] * (1 + len(pieces)),
        [pltpu.VMEM((2 * total, n), BF16)],
        vmem=12,
        cost=0.8,
    )(*scalars, inverse, *pieces)


def weighted_kernel(place_ref, inverse_ref, sigma_ref, totals_ref, out_ref):
    _, rows, n = sigma_ref.shape
    start = pl.multiple_of(place_ref[0] * rows, rows)
    one = wide(totals_ref[0:1, LANES : 2 * LANES], n)
    offset = wide(totals_ref[0:1, 2 * LANES : 3 * LANES], n)
    sigma = sigma_ref[...].reshape(2 * rows, n)
    store(out_ref, finished_rows(sigma, inverse_ref, start, 1.0, offset, one))


def weighted_rows(place, inverse, sigma, totals):
    _, rows, n = sigma.shape
    return call(
        weighted_kernel,
        jax.ShapeDtypeStruct((2 * rows, n), BF16),
        [SMEM] + [VMEM] * 3,
        vmem=8,
        cost=0.3,
    )(place, inverse, sigma, totals)


def own_matrices_kernel(slab_ref, self_ref, partner_ref, coupling_ref, low_ref, high_ref, factor_ref, both):
    core = slab_ref[0] & 1
    both[core] = self_ref[...]
    both[1 - core] = partner_ref[...]
    coupling = coupling_ref[...]
    low_ref[...] = mxu(both[0], coupling).astype(BF16)
    high_ref[...] = mxu(both[1], coupling).astype(BF16)

    @pl.when(core == 0)
    def _():
        store(factor_ref, product(high_ref[...], self_ref[...]))

    @pl.when(core != 0)
    def _():
        factor_ref[...] = jnp.zeros_like(factor_ref)


def own_matrices(slab, own, partner, coupling):
    n = coupling.shape[0]
    matrix = jax.ShapeDtypeStruct((2 * n, n), BF16)
    return call(
        own_matrices_kernel,
        [matrix, matrix, matrix],
        [SMEM] + [VMEM] * 3,
        [pltpu.VMEM((2, 2 * n, n), BF16)],
        vmem=20,
        cost=0.0,
    )(slab, own, partner, coupling)


def far_matrices_kernel(slab_ref, chain_ref, self_ref, partner_ref, coupling_ref, high_ref, moves, factors, *more):
    core = slab_ref[0] & 1
    low, high = core, 1 - core

    def chain_and_high(high_inverse):
        step = mxu(high_inverse, coupling_ref[...]).astype(BF16)
        store(moves.at[high], product(chain_ref[...], step))

    @pl.when(core == 0)
    def _():
        chain_and_high(partner_ref[...])
        moves[low] = moves[high]
        for chain in more:
            step = mxu(self_ref[...], coupling_ref[...]).astype(BF16)
            store(chain, product(moves[high], step))

    @pl.when(core != 0)
    def _():
        moves[low] = chain_ref[...]
        for chain in more:
            chain_and_high(self_ref[...])
            step = mxu(partner_ref[...], coupling_ref[...]).astype(BF16)
            store(chain, product(moves[high], step))

    store(moves.at[high], product(high_ref[...], moves[low]))
    for place in range(2):
        store(factors.at[place], product(moves[place], self_ref[...]))


def far_matrices(slab, chain, far_self, far_partner, coupling, high, goes_on):
    n = coupling.shape[0]
    matrix = jax.ShapeDtypeStruct((2 * n, n), BF16)
    pair = jax.ShapeDtypeStruct((2, 2 * n, n), BF16)
    return call(
        far_matrices_kernel,
        [pair, pair] + [matrix] * goes_on,
        [SMEM] + [VMEM] * 5,
        vmem=24,
        cost=5.2,
    )(slab, chain, far_self, far_partner, coupling, high)


def block_start(place, group, n, energies):
    first, last = group
    size = n * (last - first) // energies
    return size, pl.multiple_of((place ^ first) // (last - first) * size, size)


def moved_rows(rows, move):
    n = move.shape[0] // 2
    return complex_of(mxu_nt(rows, move[:n]), mxu_nt(rows, move[n:]))


def moved_term(rows, move, factor):
    moved = [part.astype(BF16) for part in moved_rows(rows, move)]
    return complex_of(mxu(factor, moved[0]), mxu(factor, moved[1]))


def own_terms_kernel(place_ref, high_ref, own_ref, factor_ref, *refs, groups, energies):
    chunks, (self_ref, partner_ref, rows_ref) = refs[:-3], refs[-3:]
    n = self_ref.shape[1]
    for group, chunk in zip(groups, chunks):
        size, start = block_start(place_ref[0], group, n, energies)
        for part in range(2):
            at = pl.ds(pl.multiple_of(part * n + start, size), size)
            rows_ref[at, :] = chunk[part * size : (part + 1) * size, :]
    store(partner_ref, moved_term(rows_ref[...], high_ref[...], factor_ref[...]))
    store(self_ref, product(own_ref[...], rows_ref[...]))


def own_terms(place, high, own, factor, chunks, groups, energies):
    n = own.shape[1]
    total = jax.ShapeDtypeStruct((2 * n, n), F32)
    return call(
        functools.partial(own_terms_kernel, groups=groups, energies=energies),
        [total, total],
        [SMEM] + [VMEM] * (3 + len(chunks)),
        [pltpu.VMEM((2 * n, n), BF16)],
        vmem=20,
        cost=3.6,
    )(place, high, own, factor, *chunks)


def far_terms_kernel(place_ref, total_ref, *refs, target, group, energies):
    out_ref, refs = refs[-1], refs[:-1]
    n = total_ref.shape[1]
    total = [total_ref[:n, :], total_ref[n:, :]]
    size, start = block_start(place_ref[0], group, n, energies)
    for term in range(len(refs) // 3):
        block, moves, factors = refs[3 * term : 3 * term + 3]
        factor = factors.at[target]
        parts = moved_term(block[: 2 * size, :], moves[target], factor[:, pl.ds(start, size)])
        total = [a + b for a, b in zip(total, parts)]
    store(out_ref, total)


def far_terms(place, total, terms, group, target, dtype, energies):
    n = total.shape[1]
    arrays = [array for term in terms for array in term]
    return call(
        functools.partial(far_terms_kernel, target=target, group=group, energies=energies),
        jax.ShapeDtypeStruct((2 * n, n), dtype),
        [SMEM] + [VMEM] * (1 + len(arrays)),
        vmem=20 + 5 * (len(terms) - 1),
        cost=1.8,
    )(place, total, *arrays)


def diagonal_kernel(place_ref, inverse_ref, high_ref, factor_ref, rows_ref, *refs, rows):
    out_ref, refs = refs[-1], refs[:-1]
    n = rows_ref.shape[1]
    pick = (
        lax.broadcasted_iota(jnp.int32, (rows, n), 0) + place_ref[0] * rows
        == lax.broadcasted_iota(jnp.int32, (rows, n), 1)
    ).astype(BF16)

    def part(first, second):
        real, imag = mxu_nt(pick, first[:n]), mxu_nt(pick, first[n:])
        return jnp.sum(real * second[1] + imag * second[0], axis=0, keepdims=True)

    block = rows_ref[...]
    sums = [
        part(inverse_ref[...], (block[:rows].astype(F32), block[rows:].astype(F32))),
        part(factor_ref[...], moved_rows(block, high_ref[...])),
    ]
    for far in range(len(refs) // 3):
        far_ref, moves, factors = refs[3 * far : 3 * far + 3]
        block = far_ref[...]
        for target in range(2):
            sums[target] += part(factors[target], moved_rows(block, moves[target]))
    for target in range(2):
        out_ref[target : target + 1, :] = sums[target]


def diagonal_sums(place, inverse, high, factor, rows, far, energies):
    n = inverse.shape[1]
    arrays = [array for term in far for array in term]
    return call(
        functools.partial(diagonal_kernel, rows=n // energies),
        jax.ShapeDtypeStruct((2, n), F32),
        [SMEM] + [VMEM] * (4 + len(arrays)),
        vmem=20 + 5 * (len(far) - 1),
        cost=2.4,
    )(place, inverse, high, factor, rows, *arrays)


def add_kernel(first_ref, second_ref, out_ref):
    out_ref[...] = first_ref[...] + second_ref[...]


def add(first, second):
    shape = jax.ShapeDtypeStruct(first.shape, first.dtype)
    return call(add_kernel, shape, [VMEM] * 2, vmem=4)(first, second)


def finish_kernel(own_ref, partner_ref, own_density_ref, partner_density_ref, green_ref, density_ref):
    green_ref[...] = (own_ref[...] + partner_ref[...].astype(F32)).astype(BF16)
    density_ref[...] = -(own_density_ref[0:1, :] + partner_density_ref[1:2, :])


def finish(own, partner, own_density, partner_density):
    n = own.shape[1]
    return call(
        finish_kernel,
        [jax.ShapeDtypeStruct((2 * n, n), BF16), jax.ShapeDtypeStruct((1, n), F32)],
        [VMEM] * 4,
        cost=1.2,
    )(own, partner, own_density, partner_density)


def exchange(x, axis, distance):
    size = lax.axis_size(axis)
    return lax.ppermute(x, axis, [(i, i ^ distance) for i in range(size)])


def shift(x, axis, by):
    size = lax.axis_size(axis)
    return lax.ppermute(x, axis, [(i, i + by) for i in range(size - by)])


def after(x, *others):
    return lax.optimization_barrier((x, *others))[0]


def exchange_all(pieces, order, window):
    received = list(pieces)
    for at, distance in enumerate(order):
        piece = pieces[distance]
        if at >= window:
            piece = after(piece, received[order[at - window]])
        received[distance] = exchange(piece, "energy", distance)
    return received


def local(
    green_prev,
    slab_inverse,
    coupling_block,
    phonon_coupling,
    offset,
    occupation,
    pair_source,
    pair_mode,
    active_slabs,
):
    energies = pair_source.shape[0]
    n = coupling_block.shape[0]
    rows = n // energies
    slabs = lax.axis_size("slab")
    place = lax.axis_index("energy").astype(jnp.int32)
    slab = lax.axis_index("slab").astype(jnp.int32)
    core = slab & 1
    place_one = place[None]
    slab_one = slab[None]
    column = slab_inverse[0].reshape(2 * n, n)
    green = green_prev[0, 0]

    half = energies // 2
    partner = exchange(column, "slab", 1)
    far_selves = [shift(column, "slab", behind) for behind in range(2, slabs, 2)]
    weights = weight_rows(slab_one, active_slabs, occupation, offset, n)
    sent = [
        jnp.concatenate(
            [lax.dynamic_slice_in_dim(part, (place ^ distance) * rows, rows) for part in green]
            + [weights]
        )
        for distance in range(energies)
    ]
    sent[1] = after(sent[1], partner)
    pieces = exchange_all(sent, range(1, energies), energies)
    low_move, high_move, own_factor = own_matrices(slab_one, column, partner, coupling_block)
    pieces[0] = after(pieces[0], high_move)
    *mixed, weighted, totals = mix(place_one, pair_source, pair_mode, phonon_coupling, pieces)
    far_partners = [exchange(after(far_self, mixed[1]), "slab", 1) for far_self in far_selves]
    back = exchange_all(mixed, range(1, energies), energies)
    back[1] = after(back[1], *far_partners)

    scalars = (place_one, slab_one, active_slabs, offset)
    near, cross = (0, half), (half, energies)
    own_weighted = weighted_rows(place_one, column, weighted, totals)
    far_weighted = [shift(own_weighted, "slab", behind) for behind in range(2, slabs, 2)]
    back[0] = after(back[0], own_weighted)
    own_near = right_rows(scalars, column, back[:half], 0)

    chain = after(low_move, own_near, *far_weighted)
    far = []
    for index, (far_self, far_partner) in enumerate(zip(far_selves, far_partners)):
        moves, factors, *chain = far_matrices(
            slab_one,
            chain if index == 0 else chain[0],
            far_self,
            far_partner,
            coupling_block,
            high_move,
            index + 1 < len(far_selves),
        )
        far.append((moves, factors))
    density = diagonal_sums(
        place_one,
        column,
        high_move,
        own_factor,
        own_weighted,
        [(rows, *matrices) for rows, matrices in zip(far_weighted, far)],
        energies,
    )

    def energy_step(density, distance):
        return add(density, exchange(density, "energy", distance))

    distances = [1 << bit for bit in range(energies.bit_length() - 1)]
    early = 1
    density = after(density, back[half])
    for distance in distances[:early]:
        density = energy_step(density, distance)
    back[half] = after(back[half], density)
    own_cross = right_rows(scalars, column, back[half:], half)
    far_near = [shift(own_near, "slab", behind) for behind in range(2, slabs, 2)]
    far_cross = [shift(own_cross, "slab", behind) for behind in range(2, slabs, 2)]

    for_self, for_partner = own_terms(
        place_one, high_move, column, own_factor, [own_near, own_cross], (near, cross), energies
    )
    near_terms = [(rows, *matrices) for rows, matrices in zip(far_near, far)]
    cross_terms = [(rows, *matrices) for rows, matrices in zip(far_cross, far)]
    def far_sum(total, terms, group, target, dtype=F32):
        return far_terms(place_one, total, terms, group, target, dtype, energies) if terms else total

    for_partner = far_sum(for_partner, near_terms, near, 1)
    for_self = far_sum(for_self, near_terms, near, 0)
    for distance in distances[early:]:
        density = energy_step(density, distance)
    density_partner = exchange(after(density, for_self), "slab", 1)
    for_partner = far_sum(after(for_partner, density_partner, for_self), cross_terms, cross, 1, BF16).astype(BF16)
    from_partner = exchange(for_partner, "slab", 1)
    for_self = far_sum(for_self, cross_terms, cross, 0)
    current, density = finish(for_self, from_partner, density, density_partner)
    return (current.reshape(1, 1, 2, n, n), density)


def solution(mesh):
    in_specs = (
        P("energy", "slab", None, None, None),
        P("slab", None, None, None),
        P(),
        P(None, "energy", None),
        P("energy"),
        P("energy"),
        P(),
        P(),
        P("energy"),
    )
    out_specs = (P("energy", "slab", None, None, None), P("slab", None))
    return jax.shard_map(local, mesh=mesh, in_specs=in_specs, out_specs=out_specs, check_vma=False)
```

```python
import functools

import jax
import jax.numpy as jnp
from jax import lax
from jax.experimental import pallas as pl
from jax.experimental.pallas import tpu as pltpu
from jax.sharding import PartitionSpec as P

BF16 = jnp.bfloat16
F32 = jnp.float32
LANES = 128
MICROSECOND = 3_300_000
VMEM = pl.BlockSpec(memory_space=pltpu.VMEM)
SMEM = pl.BlockSpec(memory_space=pltpu.SMEM)


def mxu(first, second):
    return jnp.dot(first, second, preferred_element_type=F32)


def mxu_nt(first, second):
    return lax.dot_general(first, second, (((1,), (1,)), ((), ())), preferred_element_type=F32)


def call(kernel, out_shape, in_specs, scratch=(), vmem=16, cost=0.0):
    return pl.pallas_call(
        kernel,
        out_shape=out_shape,
        in_specs=in_specs,
        out_specs=jax.tree.map(lambda _: VMEM, out_shape),
        scratch_shapes=list(scratch),
        compiler_params=pltpu.CompilerParams(vmem_limit_bytes=vmem * 2**20),
        cost_estimate=pl.CostEstimate(
            flops=1024, bytes_accessed=1024 + int(cost * MICROSECOND), transcendentals=0
        ),
    )


def complex_of(by_real, by_imag):
    rows = by_real.shape[0] // 2
    return by_real[:rows] - by_imag[rows:], by_real[rows:] + by_imag[:rows]


def product(first, second):
    rows = second.shape[0] // 2
    return complex_of(mxu(first, second[:rows]), mxu(first, second[rows:]))


def store(ref, parts):
    rows = parts[0].shape[0]
    for index, part in enumerate(parts):
        ref[index * rows : (index + 1) * rows, :] = part.astype(ref.dtype)


def weight_kernel(slab_ref, active_ref, occupation_ref, offset_ref, out_ref):
    shape = out_ref.shape
    row = lax.broadcasted_iota(jnp.int32, shape, 0)
    lane = lax.broadcasted_iota(jnp.int32, shape, 1)
    weight = occupation_ref[0]
    active = jnp.where(slab_ref[0] < active_ref[0], weight, 0.0)
    rest = jnp.where(lane < 2 * LANES, weight, weight * offset_ref[0])
    rest = jnp.where(lane < LANES, active, rest)
    out = jnp.zeros(shape, F32)
    for index in range(3):
        part = rest.astype(BF16).astype(F32)
        out = jnp.where(row == index, part, out)
        rest = rest - part
    out_ref[...] = out.astype(BF16)


def weight_rows(slab, active, occupation, offset, n):
    shape = jax.ShapeDtypeStruct((8, n), BF16)
    return call(weight_kernel, shape, [SMEM] * 4, vmem=4)(slab, active, occupation, offset)


def wide(row, n):
    return jnp.concatenate([row[:, :LANES]] * (n // LANES), axis=1)


def mix_kernel(place_ref, source_ref, mode_ref, phonon_ref, *refs):
    energies = (len(refs) - 5) // 2
    pieces, outs = refs[:energies], refs[energies : 2 * energies]
    weighted_ref, totals_ref, green, phonon, weights = refs[2 * energies :]
    place = place_ref[0]
    pairs = source_ref.shape[1]
    rows, n = phonon_ref.shape[1:]
    phonon[...] = phonon_ref[...].astype(F32)
    totals = jnp.zeros((1, n), F32)
    for distance in range(energies):
        piece = pieces[distance]
        for part in range(2):
            green[place ^ distance, part] = piece[part * rows : (part + 1) * rows, :].astype(F32)
        parts = piece[2 * rows :, :].astype(F32)
        row = parts[0:1] + parts[1:2] + parts[2:3]
        totals = totals + row
        weights[place ^ distance] = jnp.broadcast_to(wide(row, n), (8, n))
    totals_ref[...] = jnp.broadcast_to(totals, totals_ref.shape)
    step = 16

    @pl.loop(0, rows // step)
    def _(block):
        at = pl.ds(pl.multiple_of(block * step, step), step)
        weighted_real = jnp.zeros((step, n), F32)
        weighted_imag = jnp.zeros((step, n), F32)
        for distance in range(energies):
            energy = place ^ distance
            real = jnp.zeros((step, n), F32)
            imag = jnp.zeros((step, n), F32)
            for pair in range(pairs):
                origin = source_ref[energy, pair]
                factor = phonon[mode_ref[energy, pair], at, :]
                real = real + factor * green[origin, 0, at, :]
                imag = imag + factor * green[origin, 1, at, :]
            outs[distance][0, at, :] = real.astype(BF16)
            outs[distance][1, at, :] = imag.astype(BF16)
            weight = weights[energy, 0:1, :]
            weighted_real = weighted_real + weight * real
            weighted_imag = weighted_imag + weight * imag
        weighted_ref[0, at, :] = weighted_real.astype(BF16)
        weighted_ref[1, at, :] = weighted_imag.astype(BF16)


def mix(place, source, mode, phonon, pieces):
    energies = len(pieces)
    _, rows, n = phonon.shape
    block = jax.ShapeDtypeStruct((2, rows, n), BF16)
    return call(
        mix_kernel,
        [block] * (energies + 1) + [jax.ShapeDtypeStruct((8, n), F32)],
        [SMEM] * 3 + [VMEM] * (energies + 1),
        [
            pltpu.VMEM((energies, 2, rows, n), F32),
            pltpu.VMEM(phonon.shape, F32),
            pltpu.VMEM((energies, 8, n), F32),
        ],
        vmem=12,
        cost=2.0,
    )(place, source, mode, phonon, *pieces)


def finished_rows(sigma, inverse_ref, start, mask, offset, one):
    size, n = sigma.shape[0] // 2, sigma.shape[1]
    eye = (
        lax.broadcasted_iota(jnp.int32, (size, n), 0) + start
        == lax.broadcasted_iota(jnp.int32, (size, n), 1)
    ).astype(F32)
    real, imag = product(sigma, inverse_ref[...])
    own_real = inverse_ref[pl.ds(start, size), :].astype(F32)
    own_imag = inverse_ref[pl.ds(pl.multiple_of(n + start, size), size), :].astype(F32)
    return mask * real + offset * own_real + one * eye, mask * imag + offset * own_imag


def right_kernel(place_ref, slab_ref, active_ref, offset_ref, inverse_ref, *refs, first):
    pieces, out_ref, rows_ref = refs[:-2], refs[-2], refs[-1]
    count = len(pieces)
    place = place_ref[0] ^ first
    rows = pieces[0].shape[1]
    total = count * rows
    for index, piece in enumerate(pieces):
        at = (place ^ index) & (count - 1)
        for part in range(2):
            rows_ref[pl.ds(pl.multiple_of(part * total + at * rows, rows), rows), :] = piece[part]
    mask = jnp.where(slab_ref[0] < active_ref[0], 1.0, 0.0)
    start = pl.multiple_of(place // count * total, total)
    store(out_ref, finished_rows(rows_ref[...], inverse_ref, start, mask, offset_ref[0], 1.0))


def right_rows(scalars, inverse, pieces, first):
    _, rows, n = pieces[0].shape
    total = rows * len(pieces)
    return call(
        functools.partial(right_kernel, first=first),
        jax.ShapeDtypeStruct((2 * total, n), BF16),
        [SMEM] * 4 + [VMEM] * (1 + len(pieces)),
        [pltpu.VMEM((2 * total, n), BF16)],
        vmem=12,
        cost=0.8,
    )(*scalars, inverse, *pieces)


def weighted_kernel(place_ref, inverse_ref, sigma_ref, totals_ref, out_ref):
    _, rows, n = sigma_ref.shape
    start = pl.multiple_of(place_ref[0] * rows, rows)
    one = wide(totals_ref[0:1, LANES : 2 * LANES], n)
    offset = wide(totals_ref[0:1, 2 * LANES : 3 * LANES], n)
    sigma = sigma_ref[...].reshape(2 * rows, n)
    store(out_ref, finished_rows(sigma, inverse_ref, start, 1.0, offset, one))


def weighted_rows(place, inverse, sigma, totals):
    _, rows, n = sigma.shape
    return call(
        weighted_kernel,
        jax.ShapeDtypeStruct((2 * rows, n), BF16),
        [SMEM] + [VMEM] * 3,
        vmem=8,
        cost=0.3,
    )(place, inverse, sigma, totals)


def own_matrices_kernel(slab_ref, self_ref, partner_ref, coupling_ref, low_ref, high_ref, factor_ref, both):
    core = slab_ref[0] & 1
    both[core] = self_ref[...]
    both[1 - core] = partner_ref[...]
    coupling = coupling_ref[...]
    low_ref[...] = mxu(both[0], coupling).astype(BF16)
    high_ref[...] = mxu(both[1], coupling).astype(BF16)

    @pl.when(core == 0)
    def _():
        store(factor_ref, product(high_ref[...], self_ref[...]))

    @pl.when(core != 0)
    def _():
        factor_ref[...] = jnp.zeros_like(factor_ref)


def own_matrices(slab, own, partner, coupling):
    n = coupling.shape[0]
    matrix = jax.ShapeDtypeStruct((2 * n, n), BF16)
    return call(
        own_matrices_kernel,
        [matrix, matrix, matrix],
        [SMEM] + [VMEM] * 3,
        [pltpu.VMEM((2, 2 * n, n), BF16)],
        vmem=20,
        cost=0.0,
    )(slab, own, partner, coupling)


def far_matrices_kernel(slab_ref, chain_ref, self_ref, partner_ref, coupling_ref, high_ref, moves, factors, *more):
    core = slab_ref[0] & 1
    low, high = core, 1 - core

    def chain_and_high(high_inverse):
        step = mxu(high_inverse, coupling_ref[...]).astype(BF16)
        store(moves.at[high], product(chain_ref[...], step))

    @pl.when(core == 0)
    def _():
        chain_and_high(partner_ref[...])
        moves[low] = moves[high]
        for chain in more:
            step = mxu(self_ref[...], coupling_ref[...]).astype(BF16)
            store(chain, product(moves[high], step))

    @pl.when(core != 0)
    def _():
        moves[low] = chain_ref[...]
        for chain in more:
            chain_and_high(self_ref[...])
            step = mxu(partner_ref[...], coupling_ref[...]).astype(BF16)
            store(chain, product(moves[high], step))

    store(moves.at[high], product(high_ref[...], moves[low]))
    for place in range(2):
        store(factors.at[place], product(moves[place], self_ref[...]))


def far_matrices(slab, chain, far_self, far_partner, coupling, high, goes_on):
    n = coupling.shape[0]
    matrix = jax.ShapeDtypeStruct((2 * n, n), BF16)
    pair = jax.ShapeDtypeStruct((2, 2 * n, n), BF16)
    return call(
        far_matrices_kernel,
        [pair, pair] + [matrix] * goes_on,
        [SMEM] + [VMEM] * 5,
        vmem=24,
        cost=5.2,
    )(slab, chain, far_self, far_partner, coupling, high)


def block_start(place, group, n, energies):
    first, last = group
    size = n * (last - first) // energies
    return size, pl.multiple_of((place ^ first) // (last - first) * size, size)


def moved_rows(rows, move):
    n = move.shape[0] // 2
    return complex_of(mxu_nt(rows, move[:n]), mxu_nt(rows, move[n:]))


def moved_term(rows, move, factor):
    moved = [part.astype(BF16) for part in moved_rows(rows, move)]
    return complex_of(mxu(factor, moved[0]), mxu(factor, moved[1]))


def own_terms_kernel(place_ref, high_ref, own_ref, factor_ref, *refs, groups, energies):
    chunks, (self_ref, partner_ref, rows_ref) = refs[:-3], refs[-3:]
    n = self_ref.shape[1]
    for group, chunk in zip(groups, chunks):
        size, start = block_start(place_ref[0], group, n, energies)
        for part in range(2):
            at = pl.ds(pl.multiple_of(part * n + start, size), size)
            rows_ref[at, :] = chunk[part * size : (part + 1) * size, :]
    store(partner_ref, moved_term(rows_ref[...], high_ref[...], factor_ref[...]))
    store(self_ref, product(own_ref[...], rows_ref[...]))


def own_terms(place, high, own, factor, chunks, groups, energies):
    n = own.shape[1]
    total = jax.ShapeDtypeStruct((2 * n, n), F32)
    return call(
        functools.partial(own_terms_kernel, groups=groups, energies=energies),
        [total, total],
        [SMEM] + [VMEM] * (3 + len(chunks)),
        [pltpu.VMEM((2 * n, n), BF16)],
        vmem=20,
        cost=3.6,
    )(place, high, own, factor, *chunks)


def far_terms_kernel(place_ref, total_ref, *refs, target, group, energies):
    out_ref, refs = refs[-1], refs[:-1]
    n = total_ref.shape[1]
    total = [total_ref[:n, :], total_ref[n:, :]]
    size, start = block_start(place_ref[0], group, n, energies)
    for term in range(len(refs) // 3):
        block, moves, factors = refs[3 * term : 3 * term + 3]
        factor = factors.at[target]
        parts = moved_term(block[: 2 * size, :], moves[target], factor[:, pl.ds(start, size)])
        total = [a + b for a, b in zip(total, parts)]
    store(out_ref, total)


def far_terms(place, total, terms, group, target, dtype, energies):
    n = total.shape[1]
    arrays = [array for term in terms for array in term]
    return call(
        functools.partial(far_terms_kernel, target=target, group=group, energies=energies),
        jax.ShapeDtypeStruct((2 * n, n), dtype),
        [SMEM] + [VMEM] * (1 + len(arrays)),
        vmem=20 + 5 * (len(terms) - 1),
        cost=1.8,
    )(place, total, *arrays)


def diagonal_kernel(place_ref, inverse_ref, high_ref, factor_ref, rows_ref, *refs, rows):
    out_ref, refs = refs[-1], refs[:-1]
    n = rows_ref.shape[1]
    pick = (
        lax.broadcasted_iota(jnp.int32, (rows, n), 0) + place_ref[0] * rows
        == lax.broadcasted_iota(jnp.int32, (rows, n), 1)
    ).astype(BF16)

    def part(first, second):
        real, imag = mxu_nt(pick, first[:n]), mxu_nt(pick, first[n:])
        return jnp.sum(real * second[1] + imag * second[0], axis=0, keepdims=True)

    block = rows_ref[...]
    sums = [
        part(inverse_ref[...], (block[:rows].astype(F32), block[rows:].astype(F32))),
        part(factor_ref[...], moved_rows(block, high_ref[...])),
    ]
    for far in range(len(refs) // 3):
        far_ref, moves, factors = refs[3 * far : 3 * far + 3]
        block = far_ref[...]
        for target in range(2):
            sums[target] += part(factors[target], moved_rows(block, moves[target]))
    for target in range(2):
        out_ref[target : target + 1, :] = sums[target]


def diagonal_sums(place, inverse, high, factor, rows, far, energies):
    n = inverse.shape[1]
    arrays = [array for term in far for array in term]
    return call(
        functools.partial(diagonal_kernel, rows=n // energies),
        jax.ShapeDtypeStruct((2, n), F32),
        [SMEM] + [VMEM] * (4 + len(arrays)),
        vmem=20 + 5 * (len(far) - 1),
        cost=2.4,
    )(place, inverse, high, factor, rows, *arrays)


def add_kernel(first_ref, second_ref, out_ref):
    out_ref[...] = first_ref[...] + second_ref[...]


def add(first, second):
    shape = jax.ShapeDtypeStruct(first.shape, first.dtype)
    return call(add_kernel, shape, [VMEM] * 2, vmem=4)(first, second)


def finish_kernel(own_ref, partner_ref, own_density_ref, partner_density_ref, green_hbm, density_ref, green, sems):
    parts = green.shape[0]
    rows = green.shape[1]
    copies = []
    for part in range(parts):
        at = slice(part * rows, (part + 1) * rows)
        green[part] = (own_ref[at, :] + partner_ref[at, :].astype(F32)).astype(BF16)
        copies.append(pltpu.make_async_copy(green.at[part], green_hbm.at[part], sems.at[part]))
        copies[-1].start()
    density_ref[...] = -(own_density_ref[0:1, :] + partner_density_ref[1:2, :])
    for copy in copies:
        copy.wait()


def finish(own, partner, own_density, partner_density):
    n = own.shape[1]
    shape = (4, n // 2, n)
    return pl.pallas_call(
        finish_kernel,
        out_shape=[jax.ShapeDtypeStruct(shape, BF16), jax.ShapeDtypeStruct((1, n), F32)],
        in_specs=[VMEM] * 4,
        out_specs=[pl.BlockSpec(memory_space=pl.ANY), VMEM],
        scratch_shapes=[pltpu.VMEM(shape, BF16), pltpu.SemaphoreType.DMA((4,))],
        compiler_params=pltpu.CompilerParams(vmem_limit_bytes=16 * 2**20),
    )(own, partner, own_density, partner_density)


def exchange(x, axis, distance):
    size = lax.axis_size(axis)
    return lax.ppermute(x, axis, [(i, i ^ distance) for i in range(size)])


def shift(x, axis, by):
    size = lax.axis_size(axis)
    return lax.ppermute(x, axis, [(i, i + by) for i in range(size - by)])


def after(x, *others):
    return lax.optimization_barrier((x, *others))[0]


def exchange_all(pieces, order, window):
    received = list(pieces)
    for at, distance in enumerate(order):
        piece = pieces[distance]
        if at >= window:
            piece = after(piece, received[order[at - window]])
        received[distance] = exchange(piece, "energy", distance)
    return received


def local(
    green_prev,
    slab_inverse,
    coupling_block,
    phonon_coupling,
    offset,
    occupation,
    pair_source,
    pair_mode,
    active_slabs,
):
    energies = pair_source.shape[0]
    n = coupling_block.shape[0]
    rows = n // energies
    slabs = lax.axis_size("slab")
    place = lax.axis_index("energy").astype(jnp.int32)
    slab = lax.axis_index("slab").astype(jnp.int32)
    core = slab & 1
    place_one = place[None]
    slab_one = slab[None]
    column = slab_inverse[0].reshape(2 * n, n)
    green = green_prev[0, 0]

    half = energies // 2
    partner = exchange(column, "slab", 1)
    far_selves = [shift(column, "slab", behind) for behind in range(2, slabs, 2)]
    weights = weight_rows(slab_one, active_slabs, occupation, offset, n)
    sent = [
        jnp.concatenate(
            [lax.dynamic_slice_in_dim(part, (place ^ distance) * rows, rows) for part in green]
            + [weights]
        )
        for distance in range(energies)
    ]
    sent[1] = after(sent[1], partner)
    pieces = exchange_all(sent, range(1, energies), energies)
    low_move, high_move, own_factor = own_matrices(slab_one, column, partner, coupling_block)
    pieces[0] = after(pieces[0], high_move)
    *mixed, weighted, totals = mix(place_one, pair_source, pair_mode, phonon_coupling, pieces)
    far_partners = [exchange(after(far_self, mixed[1]), "slab", 1) for far_self in far_selves]
    back = exchange_all(mixed, range(1, energies), energies)
    back[1] = after(back[1], *far_partners)

    scalars = (place_one, slab_one, active_slabs, offset)
    near, cross = (0, half), (half, energies)
    own_weighted = weighted_rows(place_one, column, weighted, totals)
    far_weighted = [shift(own_weighted, "slab", behind) for behind in range(2, slabs, 2)]
    back[0] = after(back[0], own_weighted)
    own_near = right_rows(scalars, column, back[:half], 0)

    chain = after(low_move, own_near, *far_weighted)
    far = []
    for index, (far_self, far_partner) in enumerate(zip(far_selves, far_partners)):
        moves, factors, *chain = far_matrices(
            slab_one,
            chain if index == 0 else chain[0],
            far_self,
            far_partner,
            coupling_block,
            high_move,
            index + 1 < len(far_selves),
        )
        far.append((moves, factors))
    density = diagonal_sums(
        place_one,
        column,
        high_move,
        own_factor,
        own_weighted,
        [(rows, *matrices) for rows, matrices in zip(far_weighted, far)],
        energies,
    )

    def energy_step(density, distance):
        return add(density, exchange(density, "energy", distance))

    distances = [1 << bit for bit in range(energies.bit_length() - 1)]
    early = 1
    density = after(density, back[half])
    for distance in distances[:early]:
        density = energy_step(density, distance)
    back[half] = after(back[half], density)
    own_cross = right_rows(scalars, column, back[half:], half)
    far_near = [shift(own_near, "slab", behind) for behind in range(2, slabs, 2)]
    far_cross = [shift(own_cross, "slab", behind) for behind in range(2, slabs, 2)]

    for_self, for_partner = own_terms(
        place_one, high_move, column, own_factor, [own_near, own_cross], (near, cross), energies
    )
    near_terms = [(rows, *matrices) for rows, matrices in zip(far_near, far)]
    cross_terms = [(rows, *matrices) for rows, matrices in zip(far_cross, far)]
    def far_sum(total, terms, group, target, dtype=F32):
        return far_terms(place_one, total, terms, group, target, dtype, energies) if terms else total

    for_partner = far_sum(for_partner, near_terms, near, 1)
    for_self = far_sum(for_self, near_terms, near, 0)
    for distance in distances[early:]:
        density = energy_step(density, distance)
    density_partner = exchange(after(density, for_self), "slab", 1)
    for_partner = far_sum(after(for_partner, density_partner, for_self), cross_terms, cross, 1, BF16).astype(BF16)
    from_partner = exchange(for_partner, "slab", 1)
    for_self = far_sum(for_self, cross_terms, cross, 0)
    current, density = finish(for_self, from_partner, density, density_partner)
    return (current.reshape(1, 1, 2, n, n), density)


def solution(mesh):
    in_specs = (
        P("energy", "slab", None, None, None),
        P("slab", None, None, None),
        P(),
        P(None, "energy", None),
        P("energy"),
        P("energy"),
        P(),
        P(),
        P("energy"),
    )
    out_specs = (P("energy", "slab", None, None, None), P("slab", None))
    return jax.shard_map(local, mesh=mesh, in_specs=in_specs, out_specs=out_specs, check_vma=False)
```
